32 devices in a mesh: stream: 16 (over z, y, core), dp: 2 (over x).
Axes of the slice: x: 2, y: 2, z: 4, core: 2. Of those that a mesh axis runs over, the one named last changes fastest.
Arguments:
- states: bfloat16 [27648, 768], P(('stream', 'dp')), may hold values from -6 to 6
- cotangent: bfloat16 [27648, 768], P(('stream', 'dp')), may hold values from -6 to 6
- word_lengths: int32 [384], replicated, may hold values from 5 to 20, as said below
- object_project: bfloat16 [768, 2304], P(None, ('stream', 'dp')), may hold values from -0.21875 to 0.21875
- object_output: bfloat16 [768, 768], P(None, ('stream', 'dp')), may hold values from -0.5 to 0.5
- object_up: bfloat16 [768, 3072], P(None, ('stream', 'dp')), may hold values from -0.21875 to 0.21875
- object_down: bfloat16 [3072, 768], P(('stream', 'dp')), may hold values from -0.109375 to 0.109375
- object_gains: bfloat16 [2, 768], P(None, ('stream', 'dp')), may hold values from 0.5 to 1.5
- cross_project: bfloat16 [768, 2304], P(None, ('stream', 'dp')), may hold values from -0.21875 to 0.21875
- cross_output: bfloat16 [768, 768], P(None, ('stream', 'dp')), may hold values from -0.5 to 0.5
- words_project: bfloat16 [768, 2304], P(None, ('stream', 'dp')), may hold values from -0.21875 to 0.21875
- words_output: bfloat16 [768, 768], P(None, ('stream', 'dp')), may hold values from -0.5 to 0.5
- region_project: bfloat16 [768, 2304], P(None, ('stream', 'dp')), may hold values from -0.21875 to 0.21875
- region_output: bfloat16 [768, 768], P(None, ('stream', 'dp')), may hold values from -0.5 to 0.5
- words_up: bfloat16 [768, 3072], P(None, ('stream', 'dp')), may hold values from -0.21875 to 0.21875
- words_down: bfloat16 [3072, 768], P(('stream', 'dp')), may hold values from -0.109375 to 0.109375
- region_up: bfloat16 [768, 3072], P(None, ('stream', 'dp')), may hold values from -0.21875 to 0.21875
- region_down: bfloat16 [3072, 768], P(('stream', 'dp')), may hold values from -0.109375 to 0.109375
- layer_gains: bfloat16 [5, 768], P(None, ('stream', 'dp')), may hold values from 0.5 to 1.5
Outputs:
- out_states: bfloat16 [27648, 768], P(('stream', 'dp'))
- grad_states: float32 [27648, 768], P(('stream', 'dp'))
- grad_object_project: float32 [768, 2304], P(None, ('stream', 'dp'))
- grad_object_output: float32 [768, 768], P(None, ('stream', 'dp'))
- grad_object_up: float32 [768, 3072], P(None, ('stream', 'dp'))
- grad_object_down: float32 [3072, 768], P(('stream', 'dp'))
- grad_object_gains: float32 [2, 768], P(None, ('stream', 'dp'))
- grad_cross_project: float32 [768, 2304], P(None, ('stream', 'dp'))
- grad_cross_output: float32 [768, 768], P(None, ('stream', 'dp'))
- grad_words_project: float32 [768, 2304], P(None, ('stream', 'dp'))
- grad_words_output: float32 [768, 768], P(None, ('stream', 'dp'))
- grad_region_project: float32 [768, 2304], P(None, ('stream', 'dp'))
- grad_region_output: float32 [768, 768], P(None, ('stream', 'dp'))
- grad_words_up: float32 [768, 3072], P(None, ('stream', 'dp'))
- grad_words_down: float32 [3072, 768], P(('stream', 'dp'))
- grad_region_up: float32 [768, 3072], P(None, ('stream', 'dp'))
- grad_region_down: float32 [3072, 768], P(('stream', 'dp'))
- grad_layer_gains: float32 [5, 768], P(None, ('stream', 'dp'))
The draws below stay inside these ranges and needn't reach their ends.
Inputs may be any that keep to these rules, and one draw needn't show every extreme that they name: Words of item i; its language positions from word_lengths[i] to 35 are padding; some item has exactly 20 words and some exactly 5.
All inputs are finite; a program needn't handle non-finite values.
Results may differ from the reference program's by a relative error of at most 0.025.
Values may be sent and summed in bfloat16 or wider, within the bound.
No kernel may reach another device: no remote copies, remote signals or barrier semaphores. Data moves between devices by JAX's collectives and lax.ppermute only.
A program may use at most 320 MiB of HBM per device.

```python
import jax
import jax.numpy as jnp
from jax import lax

D = 768
HEADS = 12
FF = 3072
HEAD = 64
SLOT = 36
WORDS = 20
ITEMS = 384
ROWS = 27648
N_STREAM = 16


def draw_word_lengths(key, part):
    key = jax.random.fold_in(key, 7)
    counts = jax.random.randint(jax.random.fold_in(key, 1), (ITEMS,), 5, WORDS + 1)
    order = jax.random.permutation(jax.random.fold_in(key, 2), ITEMS)
    counts = counts.at[order[0]].set(WORDS)
    counts = counts.at[order[1]].set(5)
    return counts.astype(jnp.int32)


def with_spikes(values, rng, source, target, parts, factor):
    def block_of(dim):
        return (jnp.arange(values.shape[dim]) // (values.shape[dim] // parts)).reshape((-1,) + (1,) * (values.ndim - 1 - dim))

    first = jax.random.permutation(rng, parts)[block_of(target)]
    second = (block_of(target) + parts // 2) % parts
    return jnp.where((block_of(source) == first) | (block_of(source) == second), factor * values, values)


def levels(rng, extent, split, least, top_value):
    factor_of, own = 1.0, jax.random.fold_in(rng, 6)
    for dim, blocks in split:
        draws = jnp.exp(jax.random.uniform(jax.random.fold_in(own, dim), (blocks,), jnp.float32, least / len(split), top_value / len(split)))
        factor_of = factor_of * jnp.repeat(draws, extent[dim] // blocks).reshape([-1 if axis == dim else 1 for axis in range(len(extent))])
    return factor_of


def gaussian(rng, shape, scale, bound, shards=(), dtype=jnp.bfloat16):
    drawn = jax.random.normal(rng, shape, jnp.float32) * scale
    if len(shards) > 0:
        drawn = levels(rng, shape, shards, -0.22, 0.18) * drawn
    return jnp.clip(drawn, min=-bound, max=bound).astype(dtype)


def heavy_noise(stream_key, shape, width, most, cuts, heavy, held_as=jnp.bfloat16):
    entries = width * jax.random.normal(stream_key, shape, jnp.float32)
    if cuts:
        entries = entries * levels(stream_key, shape, cuts, -0.22, 0.18)
    return jnp.clip(with_spikes(entries, jax.random.fold_in(stream_key, 3), *heavy), -most, most).astype(held_as)


def setup_inputs(seed: int = 0) -> dict:
    arg_keys = jax.random.split(jax.random.key(seed), 20)
    states = gaussian(arg_keys[0], (ROWS, D), 1.0, 6.0, ((0, 32),))
    cotangent = heavy_noise(arg_keys[1], (ROWS, D), 1.0, 6.0, ((0, 32),), (0, 1, 32, 2.75))
    word_lengths = draw_word_lengths(jax.random.fold_in(arg_keys[19], 71), 0)
    object_project = gaussian(arg_keys[3], (D, 3 * D), D ** -0.5, 0.21875, ((1, 32),))
    object_output = gaussian(arg_keys[4], (D, D), (D // 6) ** -0.5, 0.5, ((1, 32),))
    object_up = gaussian(arg_keys[5], (D, FF), D ** -0.5, 0.21875, ((1, 32),))
    object_down = gaussian(arg_keys[6], (FF, D), FF ** -0.5, 0.109375, ((0, 32),))
    object_gains = jnp.clip(1.0 + 0.1 * jax.random.normal(arg_keys[7], (2, D), jnp.float32), 0.5, 1.5).astype(jnp.bfloat16)
    cross_project = gaussian(arg_keys[8], (D, 3 * D), D ** -0.5, 0.21875, ((1, 32),))
    cross_output = gaussian(arg_keys[9], (D, D), (D // 6) ** -0.5, 0.5, ((1, 32),))
    words_project = gaussian(arg_keys[10], (D, 3 * D), D ** -0.5, 0.21875, ((1, 32),))
    words_output = gaussian(arg_keys[11], (D, D), (D // 6) ** -0.5, 0.5, ((1, 32),))
    region_project = gaussian(arg_keys[12], (D, 3 * D), D ** -0.5, 0.21875, ((1, 32),))
    region_output = gaussian(arg_keys[13], (D, D), (D // 6) ** -0.5, 0.5, ((1, 32),))
    words_up = gaussian(arg_keys[14], (D, FF), D ** -0.5, 0.21875, ((1, 32),))
    words_down = gaussian(arg_keys[15], (FF, D), FF ** -0.5, 0.109375, ((0, 32),))
    region_up = gaussian(arg_keys[16], (D, FF), D ** -0.5, 0.21875, ((1, 32),))
    region_down = gaussian(arg_keys[17], (FF, D), FF ** -0.5, 0.109375, ((0, 32),))
    layer_gains = jnp.clip(1.0 + 0.1 * jax.random.normal(arg_keys[18], (5, D), jnp.float32), 0.5, 1.5).astype(jnp.bfloat16)
    return {"states": states, "cotangent": cotangent, "word_lengths": word_lengths, "object_project": object_project, "object_output": object_output, "object_up": object_up, "object_down": object_down, "object_gains": object_gains, "cross_project": cross_project, "cross_output": cross_output, "words_project": words_project, "words_output": words_output, "region_project": region_project, "region_output": region_output, "words_up": words_up, "words_down": words_down, "region_up": region_up, "region_down": region_down, "layer_gains": layer_gains}


EPSILON = 1e-06
HIGH = lax.Precision.HIGHEST

@jax.custom_vjp
def low(v):
    return lax.optimization_barrier(v.astype(jnp.bfloat16)).astype(jnp.float32)

@jax.custom_vjp
def low_back(v):
    return v

def low_keep(v):
    return (low(v), None)

def low_pass(kept, grad):
    return (grad,)

def back_keep(v):
    return (v, None)

def back_low(kept, grad):
    return (low(grad),)
low.defvjp(low_keep, low_pass)
low_back.defvjp(back_keep, back_low)

def matmul(left, right):
    return jnp.dot(left, right, precision=HIGH)

def layer_norm(total, gain):
    center = total - lax.optimization_barrier(jnp.mean(total, axis=-1, keepdims=True))
    spread = lax.optimization_barrier(jnp.mean(center * center, axis=-1, keepdims=True))
    return center * lax.rsqrt(spread + EPSILON) * gain

def gelu(value):
    return 0.5 * value * (1.0 + jax.scipy.special.erf(value * 0.7071067811865476))

def attend(queries, keys, values, keep):
    count = queries.shape[0]
    query_heads = queries.reshape(count, SLOT, HEADS, HEAD)
    key_heads = keys.reshape(count, SLOT, HEADS, HEAD)
    value_heads = values.reshape(count, SLOT, HEADS, HEAD)
    scores = jnp.einsum('nahd,nbhd->nhab', query_heads, key_heads, precision=HIGH) * HEAD ** (-0.5)
    scores = low_back(scores)
    scores = jnp.where(keep[:, None, None, :], scores, -1000000000.0)
    top = lax.optimization_barrier(jnp.max(scores, axis=-1, keepdims=True))
    raised = jnp.exp(scores - top)
    weights = low(raised / lax.optimization_barrier(jnp.sum(raised, axis=-1, keepdims=True)))
    context = jnp.einsum('nhab,nbhd->nahd', weights, value_heads, precision=HIGH)
    return low(low_back(context.reshape(count, SLOT, D)))

def project(rows, weight):
    return low(low_back(matmul(rows, weight)))

def finish(rows, context, weight, gain):
    return low(layer_norm(rows + low_back(matmul(context, weight)), gain))

def self_layer(rows, weight_in, weight_out, gain, keep):
    joined = project(rows, weight_in)
    context = attend(joined[..., :D], joined[..., D:2 * D], joined[..., 2 * D:], keep)
    return finish(rows, context, weight_out, gain)

def feed_layer(rows, weight_up, weight_down, gain):
    hidden = low(gelu(low_back(matmul(rows, weight_up))))
    return low(layer_norm(rows + low_back(matmul(hidden, weight_down)), gain))

def forward(base, weights, word_lengths):
    object_project, object_output, object_up, object_down, object_gains, cross_project, cross_output, words_project, words_output, region_project, region_output, words_up, words_down, region_up, region_down, layer_gains = weights
    groups = N_STREAM // 2
    per_group = ITEMS // groups
    words = base[:ITEMS * SLOT].reshape(groups, per_group, SLOT, D)
    regions = base[ITEMS * SLOT:].reshape(groups, per_group, SLOT, D)
    lengths = word_lengths.reshape(groups, per_group)

    def one_group(pieces):
        word_rows, region_rows, group_lengths = pieces
        keep_words = jnp.arange(SLOT)[None, :] < group_lengths[:, None]
        keep_all = jnp.ones((per_group, SLOT), jnp.bool_)
        region_one = self_layer(region_rows, object_project, object_output, object_gains[0], keep_all)
        region_two = feed_layer(region_one, object_up, object_down, object_gains[1])
        word_joined = project(word_rows, cross_project)
        region_joined = project(region_two, cross_project)
        word_context = attend(word_joined[..., :D], region_joined[..., D:2 * D], region_joined[..., 2 * D:], keep_all)
        region_context = attend(region_joined[..., :D], word_joined[..., D:2 * D], word_joined[..., 2 * D:], keep_words)
        word_three = finish(word_rows, word_context, cross_output, layer_gains[0])
        region_three = finish(region_two, region_context, cross_output, layer_gains[0])
        word_four = self_layer(word_three, words_project, words_output, layer_gains[1], keep_words)
        region_four = self_layer(region_three, region_project, region_output, layer_gains[2], keep_all)
        word_five = feed_layer(word_four, words_up, words_down, layer_gains[3])
        region_five = feed_layer(region_four, region_up, region_down, layer_gains[4])
        return (word_five, region_five)
    word_out, region_out = lax.map(jax.checkpoint(one_group), (words, regions, lengths))
    return jnp.concatenate([word_out.reshape(ITEMS * SLOT, D), region_out.reshape(ITEMS * SLOT, D)], axis=0)

def reference(states, cotangent, word_lengths, object_project, object_output, object_up, object_down, object_gains, cross_project, cross_output, words_project, words_output, region_project, region_output, words_up, words_down, region_up, region_down, layer_gains):
    weights = tuple((weight.astype(jnp.float32) for weight in (object_project, object_output, object_up, object_down, object_gains, cross_project, cross_output, words_project, words_output, region_project, region_output, words_up, words_down, region_up, region_down, layer_gains)))

    def whole(base, params):
        return forward(base, params, word_lengths)
    result, pullback = jax.vjp(whole, states.astype(jnp.float32), weights)
    grad_base, grads = pullback(cotangent.astype(jnp.float32))
    return (result.astype(jnp.bfloat16), grad_base, grads[0], grads[1], grads[2], grads[3], grads[4], grads[5], grads[6], grads[7], grads[8], grads[9], grads[10], grads[11], grads[12], grads[13], grads[14], grads[15])
```

```python
import functools

import jax
import jax.numpy as jnp
from jax import lax
from jax.experimental import pallas as pl
from jax.experimental.pallas import tpu as pltpu
from jax.sharding import PartitionSpec as P

HEADS = 12
SLOT = 36
PACK = 4
EPSILON = 1e-06
MASKED = -1000000000.0
APART = -1e30
BF = jnp.bfloat16
F32 = jnp.float32
VMEM_LIMIT = 48 * 1024 * 1024

NN = (((1,), (0,)), ((), ()))
NT = (((1,), (1,)), ((), ()))
TN = (((0,), (0,)), ((), ()))


def mm(left, right, dims):
    return lax.dot_general(left, right, dims, preferred_element_type=F32)


def norm_forward(total):
    center = total - jnp.mean(total, axis=-1, keepdims=True)
    spread = jnp.mean(center * center, axis=-1, keepdims=True)
    rate = lax.rsqrt(spread + EPSILON)
    return center * rate, rate


def norm_backward(grad, normed, rate, gain):
    slope = grad * gain
    first = jnp.mean(slope, axis=-1, keepdims=True)
    second = jnp.mean(slope * normed, axis=-1, keepdims=True)
    terms = grad * normed
    rows, width = terms.shape
    return rate * (slope - first - normed * second), jnp.sum(
        terms.reshape(rows // 8, 8, width), axis=0
    )


def gelu_pair(value):
    size = jnp.abs(value) * 0.7071067811865476
    t = 1.0 / (1.0 + 0.3275911 * size)
    bell = jnp.exp(-size * size)
    poly = t * (
        0.254829592
        + t * (-0.284496736 + t * (1.421413741 + t * (-1.453152027 + t * 1.061405429)))
    )
    tail = 0.5 * poly * bell
    phi = jnp.where(value >= 0.0, 1.0 - tail, tail)
    return value * phi, phi + value * bell * 0.3989422804014327


def head_masks(width, head):
    lane = lax.broadcasted_iota(jnp.int32, (1, width), 1)
    return [jnp.where(lane // head == i, 1.0, 0.0).astype(F32) for i in range(width // head)]


def spread_heads(block, masks):
    return jnp.concatenate([block * mask.astype(block.dtype) for mask in masks], axis=0)


def fold_heads(stacked, masks):
    rows = stacked.shape[0] // len(masks)
    total = stacked[:rows] * masks[0]
    for i in range(1, len(masks)):
        total = total + stacked[i * rows : (i + 1) * rows] * masks[i]
    return total


def attend_kernel(cross, x_ref, y_ref, p_ref, o_ref, g_ref, kb_ref, apart_ref,
                  out_ref, joined_ref, probs_ref, context_ref, normed_ref, rate_ref):
    x = x_ref[...]
    width = x.shape[1]
    head = width // HEADS
    quad = 4 * head
    scale = head ** (-0.5)
    if cross:
        joined_ref[:, :width] = mm(x, p_ref[:width], NT).astype(BF)
        joined_ref[:, width:] = mm(y_ref[...], p_ref[width:], NT).astype(BF)
    else:
        joined_ref[...] = mm(x, p_ref[...], NT).astype(BF)
    masks = head_masks(quad, head)
    bias = apart_ref[...] + kb_ref[...]
    for i in range(width // quad):
        q = joined_ref[:, i * quad : (i + 1) * quad]
        k = joined_ref[:, width + i * quad : width + (i + 1) * quad]
        v = joined_ref[:, 2 * width + i * quad : 2 * width + (i + 1) * quad]
        scores = mm(k, spread_heads(q, masks), NT) * scale + bias
        raised = jnp.exp(scores - jnp.max(scores, axis=0, keepdims=True))
        probs = (raised * (1.0 / jnp.sum(raised, axis=0, keepdims=True))).astype(BF)
        probs_ref[0, i] = probs
        context_ref[:, i * quad : (i + 1) * quad] = fold_heads(mm(probs, v, TN), masks).astype(BF)
    total = x.astype(F32) + mm(context_ref[...], o_ref[...], NT)
    normed, rate = norm_forward(total)
    out_ref[...] = (normed * g_ref[...]).astype(BF)
    normed_ref[...] = normed.astype(BF)
    rate_ref[...] = rate


def whole(shape):
    return pl.BlockSpec(shape, lambda *_: (0,) * len(shape))


def attention_block(x, y, project, output, gain, key_bias, apart, cross):
    rows, width = x.shape
    block = PACK * SLOT
    groups = rows // block
    quads = HEADS // 4
    row = lambda w: pl.BlockSpec((block, w), lambda i: (i, 0))
    out, joined, probs, context, normed, rate = pl.pallas_call(
        functools.partial(attend_kernel, cross),
        grid=(groups,),
        in_specs=[
            row(width), row(width), whole(project.shape), whole(output.shape), whole((1, width)),
            row(1), whole(apart.shape),
        ],
        out_specs=[
            row(width), row(3 * width),
            pl.BlockSpec((1, quads, block, 4 * block), lambda i: (i, 0, 0, 0)),
            row(width), row(width), row(1),
        ],
        out_shape=[
            jax.ShapeDtypeStruct((rows, width), BF),
            jax.ShapeDtypeStruct((rows, 3 * width), BF),
            jax.ShapeDtypeStruct((groups, quads, block, 4 * block), BF),
            jax.ShapeDtypeStruct((rows, width), BF),
            jax.ShapeDtypeStruct((rows, width), BF),
            jax.ShapeDtypeStruct((rows, 1), F32),
        ],
        compiler_params=pltpu.CompilerParams(vmem_limit_bytes=VMEM_LIMIT),
        cost_estimate=pl.CostEstimate(
            flops=2 * rows * width * 6 * width, bytes_accessed=24 * rows * width, transcendentals=0
        ),
        name="attend",
    )(x, y, project, output, gain, key_bias, apart)
    return out, (joined, probs, context, normed, rate)


def attend_back_kernel(cross, grad_ref, normed_ref, rate_ref, g_ref, joined_ref, probs_ref, p_ref, o_ref,
                       branch_ref, dj_ref, dx_ref, *rest):
    gain_ref = rest[-1]
    width = grad_ref.shape[1]
    head = width // HEADS
    quad = 4 * head
    scale = head ** (-0.5)
    total, terms = norm_backward(
        grad_ref[...].astype(F32), normed_ref[...].astype(F32), rate_ref[...], g_ref[...]
    )

    @pl.when(pl.program_id(0) == 0)
    def _():
        gain_ref[...] = jnp.zeros_like(gain_ref)

    gain_ref[...] += terms
    branch = total.astype(BF)
    branch_ref[...] = branch
    grad_context = mm(branch, o_ref[...], NN).astype(BF)
    masks = head_masks(quad, head)
    for i in range(width // quad):
        low, high = i * quad, (i + 1) * quad
        q = joined_ref[:, low:high]
        k = joined_ref[:, width + low : width + high]
        v = joined_ref[:, 2 * width + low : 2 * width + high]
        probs = probs_ref[0, i]
        wide = probs.astype(F32)
        grad_heads = spread_heads(grad_context[:, low:high], masks)
        grad_probs = mm(v, grad_heads, NT)
        mean = jnp.sum(wide * grad_probs, axis=0, keepdims=True)
        grad_scores = (wide * (grad_probs - mean)).astype(BF)
        dj_ref[:, low:high] = (fold_heads(mm(grad_scores, k, TN), masks) * scale).astype(BF)
        dj_ref[:, width + low : width + high] = (
            mm(grad_scores, spread_heads(q, masks), NN) * scale
        ).astype(BF)
        dj_ref[:, 2 * width + low : 2 * width + high] = mm(probs, grad_heads, NN).astype(BF)
    if cross:
        dx_ref[...] = total + mm(dj_ref[:, :width], p_ref[:width], NN)
        rest[0][...] = mm(dj_ref[:, width:], p_ref[width:], NN).astype(rest[0].dtype)
    else:
        dx_ref[...] = total + mm(dj_ref[...], p_ref[...], NN)


def attention_block_backward(grad, project, output, gain, saved, cross):
    joined, probs, context, normed, rate = saved
    rows, width = normed.shape
    block = PACK * SLOT
    groups = rows // block
    quads = HEADS // 4
    row = lambda w: pl.BlockSpec((block, w), lambda i: (i, 0))
    extra_spec = [row(width)] if cross else []
    extra_shape = [jax.ShapeDtypeStruct((rows, width), F32)] if cross else []
    return pl.pallas_call(
        functools.partial(attend_back_kernel, cross),
        grid=(groups,),
        in_specs=[
            row(width), row(width), row(1), whole((1, width)), row(3 * width),
            pl.BlockSpec((1, quads, block, 4 * block), lambda i: (i, 0, 0, 0)),
            whole(project.shape), whole(output.shape),
        ],
        out_specs=[row(width), row(3 * width), row(width)] + extra_spec + [whole((8, width))],
        out_shape=[
            jax.ShapeDtypeStruct((rows, width), BF),
            jax.ShapeDtypeStruct((rows, 3 * width), BF),
            jax.ShapeDtypeStruct((rows, width), F32),
        ]
        + extra_shape
        + [jax.ShapeDtypeStruct((8, width), F32)],
        compiler_params=pltpu.CompilerParams(vmem_limit_bytes=VMEM_LIMIT),
        cost_estimate=pl.CostEstimate(
            flops=2 * rows * width * 7 * width, bytes_accessed=32 * rows * width, transcendentals=0
        ),
        name="attend_back",
    )(grad, normed, rate, gain, joined, probs, project, output)


def attend_weights_kernel(parts, dj_ref, x_ref, y_ref, branch_ref, context_ref, p_ref, o_ref):
    step = pl.program_id(0)

    @pl.when(step < parts)
    def _():
        p_ref[...] = mm(dj_ref[...], x_ref[...], TN).astype(BF)

    @pl.when((step >= parts) & (step < 3 * parts))
    def _():
        p_ref[...] = mm(dj_ref[...], y_ref[...], TN).astype(BF)

    @pl.when(step >= 3 * parts)
    def _():
        o_ref[...] = mm(branch_ref[...], context_ref[...], TN).astype(BF)


def attention_weights(dj, x, y, branch, context):
    rows, width = x.shape
    tile = 384
    parts = width // tile
    return pl.pallas_call(
        functools.partial(attend_weights_kernel, parts),
        grid=(4 * parts,),
        in_specs=[
            pl.BlockSpec((rows, tile), lambda i: (0, jnp.minimum(i, 3 * parts - 1))),
            whole(x.shape), whole(y.shape),
            pl.BlockSpec((rows, tile), lambda i: (0, jnp.maximum(i - 3 * parts, 0))),
            whole(context.shape),
        ],
        out_specs=[
            pl.BlockSpec((tile, width), lambda i: (jnp.minimum(i, 3 * parts - 1), 0)),
            pl.BlockSpec((tile, width), lambda i: (jnp.maximum(i - 3 * parts, 0), 0)),
        ],
        out_shape=[
            jax.ShapeDtypeStruct((3 * width, width), BF),
            jax.ShapeDtypeStruct((width, width), BF),
        ],
        compiler_params=pltpu.CompilerParams(vmem_limit_bytes=VMEM_LIMIT),
        cost_estimate=pl.CostEstimate(
            flops=2 * rows * width * 4 * width, bytes_accessed=16 * rows * width, transcendentals=0
        ),
        name="attend_weights",
    )(dj, x, y, branch, context)


def feed_kernel(x_ref, *refs):
    weights, (g_ref, out_ref, hidden_ref, slope_ref, normed_ref, rate_ref) = refs[:4], refs[4:]
    x = x_ref[...]
    wide = weights[0].shape[1]
    total = x.astype(F32)
    for i, weight in enumerate(weights):
        hidden, slope = gelu_pair(mm(x, weight[0], NT))
        hidden = hidden.astype(BF)
        hidden_ref[:, i * wide : (i + 1) * wide] = hidden
        slope_ref[:, i * wide : (i + 1) * wide] = slope.astype(BF)
        total = total + mm(hidden, weight[1], NN)
    normed, rate = norm_forward(total)
    out_ref[...] = (normed * g_ref[...]).astype(BF)
    normed_ref[...] = normed.astype(BF)
    rate_ref[...] = rate


def feed_block(x, weights, gain):
    rows, width = x.shape
    wide = weights[0].shape[1]
    hidden = wide * len(weights)
    block = rows // 3
    row = lambda w: pl.BlockSpec((block, w), lambda i: (i, 0))
    out, *saved = pl.pallas_call(
        feed_kernel,
        grid=(rows // block,),
        in_specs=[row(width)] + [whole(w.shape) for w in weights] + [whole((1, width))],
        out_specs=[row(width), row(hidden), row(hidden), row(width), row(1)],
        out_shape=[
            jax.ShapeDtypeStruct((rows, width), BF),
            jax.ShapeDtypeStruct((rows, hidden), BF),
            jax.ShapeDtypeStruct((rows, hidden), BF),
            jax.ShapeDtypeStruct((rows, width), BF),
            jax.ShapeDtypeStruct((rows, 1), F32),
        ],
        compiler_params=pltpu.CompilerParams(vmem_limit_bytes=VMEM_LIMIT),
        cost_estimate=pl.CostEstimate(
            flops=4 * rows * width * hidden, bytes_accessed=4 * (rows + width) * hidden, transcendentals=0
        ),
        name="feed",
    )(x, *weights, gain)
    return out, tuple(saved)


def norm_back_kernel(grad_ref, normed_ref, rate_ref, g_ref, total_ref, branch_ref, gain_ref):
    total, terms = norm_backward(
        grad_ref[...].astype(F32), normed_ref[...].astype(F32), rate_ref[...], g_ref[...]
    )

    @pl.when(pl.program_id(0) == 0)
    def _():
        gain_ref[...] = jnp.zeros_like(gain_ref)

    gain_ref[...] += terms
    total_ref[...] = total
    branch_ref[...] = total.astype(BF)


def norm_block_backward(grad, normed, rate, gain):
    rows, width = normed.shape
    block = rows // 3
    row = lambda w: pl.BlockSpec((block, w), lambda i: (i, 0))
    return pl.pallas_call(
        norm_back_kernel,
        grid=(rows // block,),
        in_specs=[row(width), row(width), row(1), whole((1, width))],
        out_specs=[row(width), row(width), whole((8, width))],
        out_shape=[
            jax.ShapeDtypeStruct((rows, width), F32),
            jax.ShapeDtypeStruct((rows, width), BF),
            jax.ShapeDtypeStruct((8, width), F32),
        ],
        cost_estimate=pl.CostEstimate(
            flops=10 * rows * width, bytes_accessed=12 * rows * width, transcendentals=0
        ),
        name="norm_back",
    )(grad, normed, rate, gain)


def feed_back_kernel(start_ref, branch_ref, x_ref, *refs):
    inputs, outputs = refs[:8], refs[8:]
    dx_ref = outputs[-1]

    @pl.when(pl.program_id(0) == 0)
    def _():
        dx_ref[...] = start_ref[...]

    branch = branch_ref[...]
    x = x_ref[...]
    for i in range(2):
        up_ref, down_ref, hidden_ref, slope_ref = inputs[4 * i : 4 * i + 4]
        grad_ref = outputs[i]
        grad_hidden = mm(branch, down_ref[0], NT)
        grad_raised = (grad_hidden * slope_ref[...].astype(F32)).astype(BF)
        grad_ref[0] = mm(grad_raised, x, TN).astype(BF)
        grad_ref[1] = mm(hidden_ref[...], branch, TN).astype(BF)
        dx_ref[...] += mm(grad_raised, up_ref[0], NN)


def feed_back(start, branch, x, weights, hidden, slope, first):
    rows, width = x.shape
    wide = weights[0].shape[1]
    tile = 256
    steps = wide // tile
    in_specs = [whole(start.shape), whole(branch.shape), whole(x.shape)]
    operands = [start, branch, x]
    for i, weight in enumerate(weights):
        base = (first + i) * steps
        in_specs += [
            pl.BlockSpec((1, tile, width), lambda s: (0, s, 0)),
            pl.BlockSpec((1, tile, width), lambda s: (1, s, 0)),
            pl.BlockSpec((rows, tile), lambda s, base=base: (0, base + s)),
            pl.BlockSpec((rows, tile), lambda s, base=base: (0, base + s)),
        ]
        operands += [weight, weight, hidden, slope]
    return pl.pallas_call(
        feed_back_kernel,
        grid=(steps,),
        in_specs=in_specs,
        out_specs=[pl.BlockSpec((2, tile, width), lambda s: (0, s, 0))] * 2 + [whole((rows, width))],
        out_shape=[jax.ShapeDtypeStruct((2, wide, width), BF)] * 2
        + [jax.ShapeDtypeStruct((rows, width), F32)],
        compiler_params=pltpu.CompilerParams(vmem_limit_bytes=VMEM_LIMIT),
        cost_estimate=pl.CostEstimate(
            flops=16 * rows * width * wide, bytes_accessed=30 * wide * width, transcendentals=0
        ),
        name="feed_back",
    )(*operands)


def place_kernel(table_ref, mine_ref, theirs_ref, p_ref, o_ref):
    count = mine_ref.shape[0]

    def put(i, carry):
        for source, offset in ((mine_ref, 0), (theirs_ref, count)):
            to = table_ref[offset + i]
            p_ref[to] = source[i, 0:3]
            o_ref[to] = source[i, 3]
        return carry

    lax.fori_loop(0, count, put, 0)


def in_vmem(shape):
    return pl.BlockSpec(shape, lambda: (0,) * len(shape))


def place_weights(table, mine, theirs):
    count, unit, width = mine.shape[0], mine.shape[1] // 4, mine.shape[2]
    cut = lambda a: a.reshape(count, 4, unit, width)
    project, output = pl.pallas_call(
        place_kernel,
        in_specs=[pl.BlockSpec(memory_space=pltpu.SMEM)] + [in_vmem((count, 4, unit, width))] * 2,
        out_specs=[in_vmem((2 * count, 3, unit, width)), in_vmem((2 * count, unit, width))],
        out_shape=[
            jax.ShapeDtypeStruct((2 * count, 3, unit, width), BF),
            jax.ShapeDtypeStruct((2 * count, unit, width), BF),
        ],
        compiler_params=pltpu.CompilerParams(vmem_limit_bytes=VMEM_LIMIT),
        cost_estimate=pl.CostEstimate(flops=0, bytes_accessed=32 * count * unit * width, transcendentals=0),
        name="place",
    )(table, cut(mine), cut(theirs))
    return project.reshape(-1, width), output.reshape(-1, width)


def pick_kernel(table_ref, p_ref, o_ref, mine_ref, theirs_ref):
    count = mine_ref.shape[0]

    def take(i, carry):
        for target, offset in ((mine_ref, 0), (theirs_ref, count)):
            at = table_ref[offset + i]
            target[i, 0:3] = p_ref[at]
            target[i, 3] = o_ref[at]
        return carry

    lax.fori_loop(0, count, take, 0)


def pick_weights(table, project, output):
    width = project.shape[1]
    count = table.shape[0] // 2
    unit = width // (2 * count)
    mine, theirs = pl.pallas_call(
        pick_kernel,
        in_specs=[
            pl.BlockSpec(memory_space=pltpu.SMEM),
            in_vmem((2 * count, 3, unit, width)),
            in_vmem((2 * count, unit, width)),
        ],
        out_specs=[in_vmem((count, 4, unit, width))] * 2,
        out_shape=[jax.ShapeDtypeStruct((count, 4, unit, width), BF)] * 2,
        compiler_params=pltpu.CompilerParams(vmem_limit_bytes=VMEM_LIMIT),
        cost_estimate=pl.CostEstimate(flops=0, bytes_accessed=32 * count * unit * width, transcendentals=0),
        name="pick",
    )(table, project.reshape(2 * count, 3, unit, width), output.reshape(2 * count, unit, width))
    return mine.reshape(count, 4 * unit, width), theirs.reshape(count, 4 * unit, width)


class Cube:
    def __init__(self):
        self.replicas = lax.axis_size("dp")
        self.streams = lax.axis_size("stream")
        low = self.replicas.bit_length() - 1
        bits = low + self.streams.bit_length() - 1
        self.half = bits - 1
        self.core = low
        self.inner = [b for b in range(bits) if b not in (self.half, self.core)]
        self.number = lax.axis_index("stream") * self.replicas + lax.axis_index("dp")

    def swap(self, value, bit):
        step = 1 << bit
        if step < self.replicas:
            return lax.ppermute(value, "dp", [(i, i ^ step) for i in range(self.replicas)])
        step //= self.replicas
        return lax.ppermute(value, "stream", [(i, i ^ step) for i in range(self.streams)])

    def order(self, turn):
        turn %= len(self.inner)
        return self.inner[turn:] + self.inner[:turn]

    def table(self, turn):
        stages = [self.half] + self.order(turn)
        relative = []
        for i in range(1 << len(stages)):
            relative.append(sum(1 << bit for place, bit in enumerate(stages) if i >> place & 1))
        relative += [r | 1 << self.core for r in relative]
        return self.number ^ jnp.array(relative, jnp.int32)

    def gather(self, own, other, turn, axis):
        pieces = jnp.concatenate([own, self.swap(other, self.half)], axis=axis)
        for bit in self.order(turn):
            pieces = jnp.concatenate([pieces, self.swap(pieces, bit)], axis=axis)
        return pieces, self.swap(pieces, self.core)

    def scatter(self, keep, send, turn, axis):
        total = add(keep, self.swap(send, self.core))
        for bit in reversed(self.order(turn)):
            count = total.shape[axis] // 2
            kept = lax.slice_in_dim(total, 0, count, axis=axis)
            sent = lax.slice_in_dim(total, count, 2 * count, axis=axis)
            total = add(kept, self.swap(sent, bit))
        return lax.slice_in_dim(total, 0, 1, axis=axis), lax.slice_in_dim(total, 1, 2, axis=axis)


def add(left, right):
    return (left.astype(F32) + right.astype(F32)).astype(left.dtype)


def on_device(
    states,
    cotangent,
    word_lengths,
    object_project,
    object_output,
    object_up,
    object_down,
    object_gains,
    cross_project,
    cross_output,
    words_project,
    words_output,
    region_project,
    region_output,
    words_up,
    words_down,
    region_up,
    region_down,
    layer_gains,
):
    cube = Cube()
    width = states.shape[1]
    half = cube.streams // 2
    position = lax.axis_index("stream")
    is_words = position < half
    count = states.shape[0] // SLOT
    block = position % half * cube.replicas + lax.axis_index("dp")
    lengths = lax.dynamic_slice_in_dim(word_lengths, block * count, count)
    key_bias = jnp.where(jnp.arange(SLOT)[None, :] < lengths[:, None], 0.0, MASKED).reshape(-1, 1)
    no_bias = jnp.zeros_like(key_bias)
    self_bias = jnp.where(is_words, key_bias, no_bias)
    cross_bias = jnp.where(is_words, no_bias, key_bias)
    packed = PACK * SLOT
    keys = lax.broadcasted_iota(jnp.int32, (packed, 4 * packed), 0) // SLOT
    queries = lax.broadcasted_iota(jnp.int32, (packed, 4 * packed), 1) % packed // SLOT
    apart = jnp.where(keys == queries, 0.0, APART).astype(F32)

    def attention_shard(project, output):
        return jnp.concatenate([project.T, output.T], axis=0)[None]

    def feed_shards(up, down):
        both = jnp.stack([up.T, down])
        middle = both.shape[1] // 2
        return both[:, None, :middle], both[:, None, middle:]

    def gather_layer(own, other, turn):
        attention = cube.gather(own[0], other[0], turn, 0)
        feed = tuple(cube.gather(own[i], other[i], turn + i, 1) for i in (1, 2))
        return attention, tuple(
            piece.reshape(2, -1, width) for pair in feed for piece in pair
        )

    object_shards = (attention_shard(object_project, object_output), *feed_shards(object_up, object_down))
    words_shards = (attention_shard(words_project, words_output), *feed_shards(words_up, words_down))
    region_shards = (attention_shard(region_project, region_output), *feed_shards(region_up, region_down))
    cross_shard = attention_shard(cross_project, cross_output)
    own_shards = tuple(jnp.where(is_words, w, r) for w, r in zip(words_shards, region_shards))
    other_shards = tuple(jnp.where(is_words, r, w) for w, r in zip(words_shards, region_shards))

    gain_shard = jnp.concatenate([object_gains, layer_gains], axis=0)
    kinds, span = gain_shard.shape
    gain_piece = jnp.pad(gain_shard, ((0, 8 - kinds), (0, 128 - span)))[None]
    gain_mine, gain_theirs = cube.gather(gain_piece, gain_piece, 0, 0)
    gain_table = cube.table(0)
    gain_pieces = jnp.concatenate([gain_mine, gain_theirs], axis=0)[jnp.argsort(gain_table)]
    gains = gain_pieces[:, :kinds, :span].transpose(1, 0, 2).reshape(kinds, width).astype(F32)

    (object_pair, object_feed) = gather_layer(object_shards, object_shards, 0)
    others = cube.swap(states, cube.half)
    cross_pair = cube.gather(cross_shard, cross_shard, 2, 0)
    (self_pair, self_feed) = gather_layer(own_shards, other_shards, 0)

    first_table, cross_table = cube.table(0), cube.table(2)
    object_in, object_out = place_weights(first_table, *object_pair)
    cross_in, cross_out = place_weights(cross_table, *cross_pair)
    self_in, self_out = place_weights(first_table, *self_pair)
    self_gain = jnp.where(is_words, gains[3], gains[4])[None]
    feed_gain = jnp.where(is_words, gains[5], gains[6])[None]

    language = jnp.where(is_words, states, others)
    vision = jnp.where(is_words, others, states)

    one, one_saved = attention_block(
        vision, vision, object_in, object_out, gains[0:1], no_bias, apart, False
    )
    two, two_saved = feed_block(one, object_feed, gains[1:2])
    x = jnp.where(is_words, language, two)
    y = jnp.where(is_words, two, language)
    three, three_saved = attention_block(x, y, cross_in, cross_out, gains[2:3], cross_bias, apart, True)
    four, four_saved = attention_block(
        three, three, self_in, self_out, self_gain, self_bias, apart, False
    )
    five, five_saved = feed_block(four, self_feed, feed_gain)

    def feed_backward(grad, rows, weights, gain, saved):
        hidden, slope, normed, rate = saved
        start, branch, gain_terms = norm_block_backward(grad, normed, rate, gain)
        b_keep, b_send, middle = feed_back(start, branch, rows, weights[:2], hidden, slope, 0)
        c_keep, c_send, result = feed_back(middle, branch, rows, weights[2:], hidden, slope, 2)
        return result, gain_terms, ((b_keep, b_send), (c_keep, c_send))

    def scatter_feed(pairs, turn):
        pieces = cube.replicas * cube.streams // 2
        cut = lambda a: a.reshape(2, pieces, -1, width)
        return [cube.scatter(cut(keep), cut(send), turn + i, 1) for i, (keep, send) in ((1, pairs[0]), (2, pairs[1]))]

    grad_four, feed_terms, self_feed_pairs = feed_backward(cotangent, four, self_feed, feed_gain, five_saved)
    self_feed_sums = scatter_feed(self_feed_pairs, 0)

    branch, dj, grad_three, self_terms = attention_block_backward(
        grad_four, self_in, self_out, self_gain, four_saved, False
    )
    self_sums = cube.scatter(
        *pick_weights(first_table, *attention_weights(dj, three, three, branch, four_saved[2])), 0, 0
    )

    branch, dj, grad_x, grad_y, cross_terms = attention_block_backward(
        grad_three, cross_in, cross_out, gains[2:3], three_saved, True
    )
    cross_sums = cube.scatter(
        *pick_weights(cross_table, *attention_weights(dj, x, y, branch, three_saved[2])), 2, 0
    )

    grad_two = jnp.where(is_words, grad_y, grad_x)
    grad_one, two_terms, object_feed_pairs = feed_backward(grad_two, one, object_feed, gains[1:2], two_saved)
    object_feed_sums = scatter_feed(object_feed_pairs, 0)
    branch, dj, grad_vision, one_terms = attention_block_backward(
        grad_one, object_in, object_out, gains[0:1], one_saved, False
    )
    object_sums = cube.scatter(
        *pick_weights(first_table, *attention_weights(dj, vision, vision, branch, one_saved[2])), 0, 0
    )
    sent = jnp.where(is_words, grad_vision, grad_y).astype(BF)
    received = cube.swap(sent, cube.half).astype(F32)
    grad_states = jnp.where(is_words, grad_x, grad_vision) + received

    words_side = is_words.astype(F32)
    region_side = 1.0 - words_side
    sums = [one_terms, two_terms, cross_terms, self_terms, self_terms, feed_terms, feed_terms]
    sides = [1.0, 1.0, 1.0, words_side, region_side, words_side, region_side]
    gain_sums = jnp.stack([jnp.sum(s, axis=0) * side for s, side in zip(sums, sides)])
    gain_cut = gain_sums.reshape(kinds, -1, span).transpose(1, 0, 2)
    gain_cut = jnp.pad(gain_cut, ((0, 0), (0, 8 - kinds), (0, 128 - span)))[gain_table]
    middle = gain_cut.shape[0] // 2
    gain_own, gain_other = cube.scatter(gain_cut[:middle], gain_cut[middle:], 0, 0)
    gain_grad = (gain_own + cube.swap(gain_other, cube.half))[0, :kinds, :span]

    def both(sums):
        own, other = sums
        return own.astype(F32) + cube.swap(other, cube.half).astype(F32)

    def apart_by_stream(sums):
        own, other = sums
        received = cube.swap(other, cube.half)
        return (
            jnp.where(is_words, own, received).astype(F32),
            jnp.where(is_words, received, own).astype(F32),
        )

    def attention_grads(piece):
        flat = piece[0]
        cut = 3 * flat.shape[0] // 4
        return flat[:cut].T, flat[cut:].T

    def feed_grads(first, second):
        joined = jnp.concatenate([first[:, 0], second[:, 0]], axis=1)
        return joined[0].T, joined[1]

    object_project_grad, object_output_grad = attention_grads(both(object_sums))
    object_up_grad, object_down_grad = feed_grads(*[both(s) for s in object_feed_sums])
    cross_project_grad, cross_output_grad = attention_grads(both(cross_sums))
    words_piece, region_piece = apart_by_stream(self_sums)
    words_project_grad, words_output_grad = attention_grads(words_piece)
    region_project_grad, region_output_grad = attention_grads(region_piece)
    split = [apart_by_stream(s) for s in self_feed_sums]
    words_up_grad, words_down_grad = feed_grads(split[0][0], split[1][0])
    region_up_grad, region_down_grad = feed_grads(split[0][1], split[1][1])
    return (
        five,
        grad_states,
        object_project_grad,
        object_output_grad,
        object_up_grad,
        object_down_grad,
        gain_grad[:2],
        cross_project_grad,
        cross_output_grad,
        words_project_grad,
        words_output_grad,
        region_project_grad,
        region_output_grad,
        words_up_grad,
        words_down_grad,
        region_up_grad,
        region_down_grad,
        gain_grad[2:],
    )


def solution(mesh):
    rows = P(("stream", "dp"), None)
    columns = P(None, ("stream", "dp"))
    in_specs = (
        rows, rows, P(),
        columns, columns, columns, rows, columns,
        columns, columns,
        columns, columns, columns, columns,
        columns, rows, columns, rows,
        columns,
    )
    out_specs = (
        rows, rows,
        columns, columns, columns, rows, columns,
        columns, columns,
        columns, columns, columns, columns,
        columns, rows, columns, rows,
        columns,
    )
    return jax.shard_map(
        on_device, mesh=mesh, in_specs=in_specs, out_specs=out_specs, check_vma=False
    )
```

```python
import functools

import jax
import jax.numpy as jnp
from jax import lax
from jax.experimental import pallas as pl
from jax.experimental.pallas import tpu as pltpu
from jax.sharding import PartitionSpec as P

HEADS = 12
SLOT = 36
PACK = 4
EPSILON = 1e-06
MASKED = -1000000000.0
APART = -1e30
BF = jnp.bfloat16
F32 = jnp.float32
VMEM_LIMIT = 48 * 1024 * 1024

NN = (((1,), (0,)), ((), ()))
NT = (((1,), (1,)), ((), ()))
TN = (((0,), (0,)), ((), ()))


def mm(left, right, dims):
    return lax.dot_general(left, right, dims, preferred_element_type=F32)


def norm_forward(total):
    center = total - jnp.mean(total, axis=-1, keepdims=True)
    spread = jnp.mean(center * center, axis=-1, keepdims=True)
    rate = lax.rsqrt(spread + EPSILON)
    return center * rate, rate


def norm_backward(grad, normed, rate, gain):
    slope = grad * gain
    first = jnp.mean(slope, axis=-1, keepdims=True)
    second = jnp.mean(slope * normed, axis=-1, keepdims=True)
    terms = grad * normed
    rows, width = terms.shape
    return rate * (slope - first - normed * second), jnp.sum(
        terms.reshape(rows // 8, 8, width), axis=0
    )


def gelu_pair(value):
    size = jnp.abs(value) * 0.7071067811865476
    t = 1.0 / (1.0 + 0.3275911 * size)
    bell = jnp.exp(-size * size)
    poly = t * (
        0.254829592
        + t * (-0.284496736 + t * (1.421413741 + t * (-1.453152027 + t * 1.061405429)))
    )
    tail = 0.5 * poly * bell
    phi = jnp.where(value >= 0.0, 1.0 - tail, tail)
    return value * phi, phi + value * bell * 0.3989422804014327


def head_masks(width, head):
    lane = lax.broadcasted_iota(jnp.int32, (1, width), 1)
    return [jnp.where(lane // head == i, 1.0, 0.0).astype(F32) for i in range(width // head)]


def spread_heads(block, masks):
    return jnp.concatenate([block * mask.astype(block.dtype) for mask in masks], axis=0)


def fold_heads(stacked, masks):
    rows = stacked.shape[0] // len(masks)
    total = stacked[:rows] * masks[0]
    for i in range(1, len(masks)):
        total = total + stacked[i * rows : (i + 1) * rows] * masks[i]
    return total


def attend_kernel(cross, x_ref, y_ref, p_ref, o_ref, g_ref, kb_ref, apart_ref,
                  out_ref, joined_ref, probs_ref, context_ref, normed_ref, rate_ref):
    x = x_ref[...]
    width = x.shape[1]
    head = width // HEADS
    quad = 4 * head
    scale = head ** (-0.5)
    if cross:
        joined_ref[:, :width] = mm(x, p_ref[:width], NT).astype(BF)
        joined_ref[:, width:] = mm(y_ref[...], p_ref[width:], NT).astype(BF)
    else:
        joined_ref[...] = mm(x, p_ref[...], NT).astype(BF)
    masks = head_masks(quad, head)
    group = PACK * SLOT
    for g in range(x.shape[0] // group):
        rows = slice(g * group, (g + 1) * group)
        bias = apart_ref[...] + kb_ref[rows]
        for i in range(width // quad):
            q = joined_ref[rows, i * quad : (i + 1) * quad]
            k = joined_ref[rows, width + i * quad : width + (i + 1) * quad]
            v = joined_ref[rows, 2 * width + i * quad : 2 * width + (i + 1) * quad]
            scores = mm(k, spread_heads(q, masks), NT) * scale + bias
            raised = jnp.exp(scores - jnp.max(scores, axis=0, keepdims=True))
            probs = (raised * (1.0 / jnp.sum(raised, axis=0, keepdims=True))).astype(BF)
            probs_ref[g, i] = probs
            context_ref[rows, i * quad : (i + 1) * quad] = fold_heads(mm(probs, v, TN), masks).astype(BF)
    total = x.astype(F32) + mm(context_ref[...], o_ref[...], NT)
    normed, rate = norm_forward(total)
    out_ref[...] = (normed * g_ref[...]).astype(BF)
    normed_ref[...] = normed.astype(BF)
    rate_ref[...] = rate


def whole(shape):
    return pl.BlockSpec(shape, lambda *_: (0,) * len(shape))


def in_vmem(shape):
    return pl.BlockSpec(shape, lambda: (0,) * len(shape))


def attention_block(x, y, project, output, gain, key_bias, apart, cross):
    rows, width = x.shape
    group = PACK * SLOT
    groups = rows // group
    steps = groups // 2 if groups % 2 == 0 else groups
    block = rows // steps
    quads = HEADS // 4
    probs_block = pl.BlockSpec((groups // steps, quads, group, 4 * group), lambda i: (i, 0, 0, 0))
    row = lambda w: pl.BlockSpec((block, w), lambda i: (i, 0))
    out, joined, probs, context, normed, rate = pl.pallas_call(
        functools.partial(attend_kernel, cross),
        grid=(steps,),
        in_specs=[
            row(width), row(width), whole(project.shape), whole(output.shape), whole((1, width)),
            row(1), whole(apart.shape),
        ],
        out_specs=[
            row(width), row(3 * width),
            probs_block,
            row(width), row(width), row(1),
        ],
        out_shape=[
            jax.ShapeDtypeStruct((rows, width), BF),
            jax.ShapeDtypeStruct((rows, 3 * width), BF),
            jax.ShapeDtypeStruct((groups, quads, group, 4 * group), BF),
            jax.ShapeDtypeStruct((rows, width), BF),
            jax.ShapeDtypeStruct((rows, width), BF),
            jax.ShapeDtypeStruct((rows, 1), F32),
        ],
        compiler_params=pltpu.CompilerParams(vmem_limit_bytes=VMEM_LIMIT),
        cost_estimate=pl.CostEstimate(
            flops=2 * rows * width * 6 * width, bytes_accessed=24 * rows * width, transcendentals=0
        ),
        name="attend",
    )(x, y, project, output, gain, key_bias, apart)
    return out, (joined, probs, context, normed, rate)


def attend_back_kernel(cross, grad_ref, normed_ref, rate_ref, g_ref, joined_ref, probs_ref, p_ref, o_ref,
                       *rest):
    if cross:
        side_ref, branch_ref, dj_ref, dx_ref, dy_ref, gain_ref = rest
    else:
        branch_ref, dj_ref, dx_ref, gain_ref = rest
    width = grad_ref.shape[1]
    head = width // HEADS
    quad = 4 * head
    scale = head ** (-0.5)
    total, terms = norm_backward(
        grad_ref[...].astype(F32), normed_ref[...].astype(F32), rate_ref[...], g_ref[...]
    )

    @pl.when(pl.program_id(0) == 0)
    def _():
        gain_ref[...] = jnp.zeros_like(gain_ref)

    gain_ref[...] += terms
    branch = total.astype(BF)
    branch_ref[...] = branch
    grad_context = mm(branch, o_ref[...], NN).astype(BF)
    masks = head_masks(quad, head)
    group = PACK * SLOT
    for g in range(grad_context.shape[0] // group):
        rows = slice(g * group, (g + 1) * group)
        for i in range(width // quad):
            low, high = i * quad, (i + 1) * quad
            q = joined_ref[rows, low:high]
            k = joined_ref[rows, width + low : width + high]
            v = joined_ref[rows, 2 * width + low : 2 * width + high]
            probs = probs_ref[g, i]
            wide = probs.astype(F32)
            grad_heads = spread_heads(grad_context[rows, low:high], masks)
            grad_probs = mm(v, grad_heads, NT)
            mean = jnp.sum(wide * grad_probs, axis=0, keepdims=True)
            grad_scores = (wide * (grad_probs - mean)).astype(BF)
            dj_ref[rows, low:high] = (fold_heads(mm(grad_scores, k, TN), masks) * scale).astype(BF)
            dj_ref[rows, width + low : width + high] = (
                mm(grad_scores, spread_heads(q, masks), NN) * scale
            ).astype(BF)
            dj_ref[rows, 2 * width + low : 2 * width + high] = mm(probs, grad_heads, NN).astype(BF)
    if cross:
        dx = total + mm(dj_ref[:, :width], p_ref[:width], NN)
        dy = mm(dj_ref[:, width:], p_ref[width:], NN)
        words = side_ref[0] == 1
        dx_ref[...] = jnp.where(words, dx, dy)
        dy_ref[...] = jnp.where(words, dy, dx)
    else:
        dx_ref[...] = total + mm(dj_ref[...], p_ref[...], NN)


def attention_block_backward(grad, project, output, gain, saved, side=None):
    cross = side is not None
    joined, probs, context, normed, rate = saved
    rows, width = normed.shape
    group = PACK * SLOT
    groups = rows // group
    steps = groups // 2 if groups % 2 == 0 else groups
    block = rows // steps
    quads = HEADS // 4
    probs_block = pl.BlockSpec((groups // steps, quads, group, 4 * group), lambda i: (i, 0, 0, 0))
    row = lambda w: pl.BlockSpec((block, w), lambda i: (i, 0))
    extra_spec = [row(width)] if cross else []
    extra_shape = [jax.ShapeDtypeStruct((rows, width), F32)] if cross else []
    return pl.pallas_call(
        functools.partial(attend_back_kernel, cross),
        grid=(steps,),
        in_specs=[
            row(width), row(width), row(1), whole((1, width)), row(3 * width),
            probs_block,
            whole(project.shape), whole(output.shape),
        ]
        + [pl.BlockSpec(memory_space=pltpu.SMEM)] * cross,
        out_specs=[row(width), row(3 * width), row(width)] + extra_spec + [whole((8, width))],
        out_shape=[
            jax.ShapeDtypeStruct((rows, width), BF),
            jax.ShapeDtypeStruct((rows, 3 * width), BF),
            jax.ShapeDtypeStruct((rows, width), F32),
        ]
        + extra_shape
        + [jax.ShapeDtypeStruct((8, width), F32)],
        compiler_params=pltpu.CompilerParams(vmem_limit_bytes=VMEM_LIMIT),
        cost_estimate=pl.CostEstimate(
            flops=2 * rows * width * 7 * width, bytes_accessed=32 * rows * width, transcendentals=0
        ),
        name="attend_back",
    )(grad, normed, rate, gain, joined, probs, project, output, *([side] if cross else []))


def attend_weights_kernel(parts, extra, *refs):
    tables, (dj_ref, x_ref, y_ref, branch_ref, context_ref) = refs[:parts], refs[parts : parts + 5]
    extra_ref = refs[parts + 5] if extra else None
    outputs, total = refs[parts + 5 + extra : -1], refs[-1]
    width = x_ref.shape[1]
    total[:width] = mm(dj_ref[:, :width], x_ref[...], TN)
    total[width : 3 * width] = mm(dj_ref[:, width:], y_ref[...], TN)
    total[3 * width :] = mm(branch_ref[...], context_ref[...], TN)
    for part in range(parts):
        mine_ref, theirs_ref = outputs[2 * part : 2 * part + 2]
        count = mine_ref.shape[0]
        unit = width // (2 * count)
        first, last = part * 4 * unit // parts, (part + 1) * 4 * unit // parts

        def take(i, carry):
            for target, offset in ((mine_ref, 0), (theirs_ref, count)):
                at = tables[part][offset + i]
                filled = 0
                for start, size, base in ((0, 3 * unit, 0), (3 * unit, unit, 3 * width)):
                    low, high = max(first, start), min(last, start + size)
                    if low < high:
                        row = pl.multiple_of(base + at * size + low - start, 8)
                        block = total[pl.ds(row, high - low)].reshape(-1, 8, width)
                        target[i, filled : filled + block.shape[0]] = block.astype(BF)
                        filled += block.shape[0]
                if extra and part == 0:
                    target[i, filled] = extra_ref[at].astype(BF)
            return carry

        lax.fori_loop(0, count, take, 0)


def attention_weights(tables, dj, x, y, branch, context, extra=None):
    rows, width = x.shape
    count = tables[0].shape[0] // 2
    unit = width // (2 * count)
    parts = len(tables)
    units = 4 * unit // 8 // parts
    if unit % 8:
        project = jnp.concatenate([mm(dj[:, :width], x, TN), mm(dj[:, width:], y, TN)], axis=0)
        project = project.astype(BF).reshape(2 * count, 3 * unit, width)
        output = mm(branch, context, TN).astype(BF).reshape(2 * count, unit, width)
        joined = jnp.concatenate([project, output], axis=1).reshape(2 * count, units * parts, 8, width)
        pairs = []
        for part, table in enumerate(tables):
            piece = joined[:, part * units : (part + 1) * units]
            if extra is not None and part == 0:
                piece = jnp.concatenate([piece, extra[:, None].astype(BF)], axis=1)
            piece = piece[table]
            pairs.append((piece[:count], piece[count:]))
        return pairs
    more = [] if extra is None else [extra]
    shapes = [(count, units + (len(more) if part == 0 else 0), 8, width) for part in range(parts) for _ in (0, 1)]
    outputs = pl.pallas_call(
        functools.partial(attend_weights_kernel, parts, len(more)),
        in_specs=[pl.BlockSpec(memory_space=pltpu.SMEM)] * parts
        + [in_vmem(a.shape) for a in (dj, x, y, branch, context, *more)],
        out_specs=[in_vmem(shape) for shape in shapes],
        out_shape=[jax.ShapeDtypeStruct(shape, BF) for shape in shapes],
        scratch_shapes=[pltpu.VMEM((4 * width, width), F32)],
        compiler_params=pltpu.CompilerParams(vmem_limit_bytes=VMEM_LIMIT),
        cost_estimate=pl.CostEstimate(
            flops=2 * rows * width * 4 * width, bytes_accessed=16 * rows * width, transcendentals=0
        ),
        name="attend_weights",
    )(*tables, dj, x, y, branch, context, *more)
    return [tuple(outputs[2 * part : 2 * part + 2]) for part in range(parts)]


def flat(block):
    return block.reshape(-1, block.shape[-1])


def feed_operands(weight, unit, steps):
    pieces, _, width = weight.shape
    if unit % 16 == 0:
        block = (pieces // steps, unit, width)
        return [weight, weight], [
            pl.BlockSpec(block, lambda s: (s % steps, 0, 0)),
            pl.BlockSpec(block, lambda s: (s % steps, 1, 0)),
        ]
    arrays = [weight[:, i * unit : (i + 1) * unit].reshape(steps, -1, width) for i in (0, 1)]
    return arrays, [pl.BlockSpec((1,) + arrays[0].shape[1:], lambda s: (s % steps, 0, 0))] * 2


def feed_kernel(x_ref, *refs):
    weights, (g_ref, out_ref, hidden_ref, slope_ref, normed_ref, rate_ref) = refs[:8], refs[8:]
    x = x_ref[...]
    wide = weights[0].shape[0] * weights[0].shape[1]
    total = x.astype(F32)
    for i in range(4):
        hidden, slope = gelu_pair(mm(x, flat(weights[2 * i][...]), NT))
        hidden = hidden.astype(BF)
        hidden_ref[:, i * wide : (i + 1) * wide] = hidden
        slope_ref[:, i * wide : (i + 1) * wide] = slope.astype(BF)
        total = total + mm(hidden, flat(weights[2 * i + 1][...]), NN)
    normed, rate = norm_forward(total)
    out_ref[...] = (normed * g_ref[...]).astype(BF)
    normed_ref[...] = normed.astype(BF)
    rate_ref[...] = rate


def feed_block(x, weights, unit, gain):
    rows, width = x.shape
    hidden = weights[0].shape[0] * unit * len(weights)
    parts = [feed_operands(weight, unit, 1) for weight in weights]
    block = rows // 3
    row = lambda w: pl.BlockSpec((block, w), lambda i: (i, 0))
    out, *saved = pl.pallas_call(
        feed_kernel,
        grid=(rows // block,),
        in_specs=[row(width)] + [spec for _, specs in parts for spec in specs] + [whole((1, width))],
        out_specs=[row(width), row(hidden), row(hidden), row(width), row(1)],
        out_shape=[
            jax.ShapeDtypeStruct((rows, width), BF),
            jax.ShapeDtypeStruct((rows, hidden), BF),
            jax.ShapeDtypeStruct((rows, hidden), BF),
            jax.ShapeDtypeStruct((rows, width), BF),
            jax.ShapeDtypeStruct((rows, 1), F32),
        ],
        compiler_params=pltpu.CompilerParams(vmem_limit_bytes=VMEM_LIMIT),
        cost_estimate=pl.CostEstimate(
            flops=4 * rows * width * hidden, bytes_accessed=4 * (rows + width) * hidden, transcendentals=0
        ),
        name="feed",
    )(x, *[array for arrays, _ in parts for array in arrays], gain)
    return out, tuple(saved)


def feed_back_kernel(first, *refs):
    if first:
        grad_ref, normed_ref, rate_ref, g_ref, x_ref, *refs = refs
        inputs, (branch_ref, gain_ref, *outputs) = refs[:8], refs[8:]
    else:
        start_ref, branch_ref, x_ref, *refs = refs
        inputs, outputs = refs[:8], refs[8:]
    dx_ref = outputs[-1]

    @pl.when(pl.program_id(0) == 0)
    def _():
        if first:
            total, gain_ref[...] = norm_backward(
                grad_ref[...].astype(F32), normed_ref[...].astype(F32), rate_ref[...], g_ref[...]
            )
            dx_ref[...] = total
            branch_ref[...] = total.astype(BF)
        else:
            dx_ref[...] = start_ref[...]

    branch = branch_ref[...]
    x = x_ref[...]
    for i in range(2):
        up_ref, down_ref, hidden_ref, slope_ref = inputs[4 * i : 4 * i + 4]
        grad_ref = outputs[i]
        pieces, _, unit, width = grad_ref.shape
        grad_hidden = mm(branch, flat(down_ref[...]), NT)
        grad_raised = (grad_hidden * slope_ref[...].astype(F32)).astype(BF)
        grad_ref[:, 0] = mm(grad_raised, x, TN).astype(BF).reshape(pieces, unit, width)
        grad_ref[:, 1] = mm(hidden_ref[...], branch, TN).astype(BF).reshape(pieces, unit, width)
        dx_ref[...] += mm(grad_raised, flat(up_ref[...]), NN)


def feed_back(start, x, weights, unit, hidden, slope, quarter):
    rows, width = x.shape
    first = len(start) == 4
    pieces = weights[0].shape[0]
    steps = 2 if pieces * unit // 2 % 128 == 0 else 1
    tile = pieces * unit // steps
    specs = [whole(a.shape) for a in (*start, x)]
    operands = [*start, x]
    cut = pl.BlockSpec((pieces // steps, 2, unit, width), lambda s: (s, 0, 0, 0))
    for i, weight in enumerate(weights):
        columns = pl.BlockSpec((rows, tile), lambda s, base=(quarter + i) * steps: (0, base + s))
        arrays, blocks = feed_operands(weight, unit, steps)
        specs += [*blocks, columns, columns]
        operands += [*arrays, hidden, slope]
    out_specs = [cut, cut, whole((rows, width))]
    out_shape = [jax.ShapeDtypeStruct((pieces, 2, unit, width), BF)] * 2
    out_shape += [jax.ShapeDtypeStruct((rows, width), F32)]
    if first:
        out_specs = [whole((rows, width)), whole((8, width))] + out_specs
        out_shape = [jax.ShapeDtypeStruct((rows, width), BF), jax.ShapeDtypeStruct((8, width), F32)] + out_shape
    return pl.pallas_call(
        functools.partial(feed_back_kernel, first),
        grid=(steps,),
        in_specs=specs,
        out_specs=out_specs,
        out_shape=out_shape,
        compiler_params=pltpu.CompilerParams(vmem_limit_bytes=VMEM_LIMIT),
        cost_estimate=pl.CostEstimate(
            flops=16 * rows * width * pieces * unit, bytes_accessed=30 * pieces * unit * width, transcendentals=0
        ),
        name="feed_back",
    )(*operands)


def place_kernel(parts, rows, extra, *refs):
    tables, sources, (p_ref, o_ref, *more) = refs[:parts], refs[parts : 3 * parts], refs[3 * parts :]
    count = sources[0].shape[0]
    unit = o_ref.shape[1]

    def put(device, carry):
        found = []
        for part in range(parts):
            mine_ref, theirs_ref = sources[2 * part : 2 * part + 2]
            at = tables[part][device]
            mine = mine_ref[jnp.minimum(at, count - 1)].astype(F32)
            theirs = theirs_ref[jnp.maximum(at - count, 0)].astype(F32)
            found.append(jnp.where(at < count, mine, theirs))
        piece = found[0] if parts == 1 else jnp.concatenate(found, axis=0)
        p_ref[device] = piece[: 3 * unit].astype(BF)
        o_ref[device] = piece[3 * unit : 4 * unit].astype(BF)
        if extra:
            more[0][device] = piece[4 * unit :]
        return carry

    lax.fori_loop(0, 2 * count, put, 0)


def place_weights(tables, pairs, skip, extra=0):
    parts = len(pairs)
    count, _, width = pairs[0][0].shape
    unit = width // (2 * count)
    rows = 4 * unit // parts + extra
    places = [jnp.argsort(table) for table in tables]
    if unit % 8:
        pieces = [
            jnp.concatenate(pair, axis=0)[place, skip : skip + rows]
            for pair, place, skip in zip(pairs, places, skip)
        ]
        joined = jnp.concatenate(pieces, axis=1)
        made = [joined[:, : 3 * unit], joined[:, 3 * unit : 4 * unit], joined[:, 4 * unit :].astype(F32)]
    else:
        shapes = [(2 * count, 3 * unit, width), (2 * count, unit, width)] + [(2 * count, extra, width)] * (extra > 0)
        specs = []
        for offset in skip:
            block = pl.BlockSpec((count, rows, width), lambda i, at=offset // rows: (0, at, 0))
            specs += [block, block]
        made = pl.pallas_call(
            functools.partial(place_kernel, parts, rows, extra),
            grid=(1,),
            in_specs=[pl.BlockSpec(memory_space=pltpu.SMEM)] * parts + specs,
            out_specs=[whole(shape) for shape in shapes],
            out_shape=[jax.ShapeDtypeStruct(shape, F32 if i == 2 else BF) for i, shape in enumerate(shapes)],
            compiler_params=pltpu.CompilerParams(vmem_limit_bytes=VMEM_LIMIT),
            cost_estimate=pl.CostEstimate(flops=0, bytes_accessed=16 * width * width, transcendentals=0),
            name="place",
        )(*places, *[piece for pair in pairs for piece in pair])
    project, output = made[0].reshape(-1, width), made[1].reshape(-1, width)
    return (project, output, made[2]) if extra else (project, output)


class Cube:
    def __init__(self):
        self.replicas = lax.axis_size("dp")
        self.streams = lax.axis_size("stream")
        low = self.replicas.bit_length() - 1
        bits = low + self.streams.bit_length() - 1
        self.half = bits - 1
        self.core = low
        self.inner = [b for b in range(bits) if b not in (self.half, self.core)]
        self.number = lax.axis_index("stream") * self.replicas + lax.axis_index("dp")

    def swap(self, value, bit):
        step = 1 << bit
        if step < self.replicas:
            return lax.ppermute(value, "dp", [(i, i ^ step) for i in range(self.replicas)])
        step //= self.replicas
        return lax.ppermute(value, "stream", [(i, i ^ step) for i in range(self.streams)])

    def order(self, turn):
        turn %= len(self.inner)
        return self.inner[turn:] + self.inner[:turn]

    def pieces(self, stages):
        order = stages[::-1]
        relative = [
            sum(1 << bit for place, bit in enumerate(order) if i >> place & 1) for i in range(1 << len(order))
        ]
        return self.number ^ jnp.array(relative, jnp.int32)

    def table(self, order):
        return self.pieces([self.core] + order[::-1] + [self.half])


def after(value, *others):
    return lax.optimization_barrier((value,) + others)[0]


class Gather:
    def __init__(self, cube, own, other, order):
        self.cube, self.pieces = cube, own
        self.stages = [cube.half] + order + [cube.core]
        self.sent, self.got, self.done = other, None, 0

    def advance(self, *others):
        if self.done:
            pieces, got = self.pieces, self.got
            if others:
                pieces, got, *_ = lax.optimization_barrier((pieces, got, *others))
            self.sent = self.pieces = jnp.concatenate([pieces, got], axis=0)
        elif others:
            self.sent = after(self.sent, *others)
        self.got = self.cube.swap(self.sent, self.stages[self.done])
        self.done += 1

    def pair(self):
        return self.pieces, self.got


class Scatter:
    def __init__(self, cube, keep, send, order):
        self.cube = cube
        self.stages = [cube.core] + order[::-1] + [cube.half]
        self.kept, self.sent, self.got, self.done = keep, send, None, 0

    def advance(self, *others):
        if self.done:
            kept, got = self.kept, self.got
            if others:
                kept, got, *_ = lax.optimization_barrier((kept, got, *others))
            if self.done == len(self.stages):
                self.kept, self.got, self.sent = kept, got, got
                return
            count = kept.shape[0] // 2
            self.sent = add(kept[count:], got[count:])
            self.kept = add(kept[:count], got[:count])
        self.got = self.cube.swap(self.sent, self.stages[self.done])
        self.done += 1

    def finish(self, *others):
        while self.done < len(self.stages):
            self.advance()
        self.advance(*others)
        return self.kept.astype(F32), self.got.astype(F32)


def beside(value, *chains):
    for chain in chains:
        chain.advance(value)
    return after(value, *[chain.sent for chain in chains])


def add(left, right):
    return (left.astype(F32) + right.astype(F32)).astype(left.dtype)


def on_device(
    states,
    cotangent,
    word_lengths,
    object_project,
    object_output,
    object_up,
    object_down,
    object_gains,
    cross_project,
    cross_output,
    words_project,
    words_output,
    region_project,
    region_output,
    words_up,
    words_down,
    region_up,
    region_down,
    layer_gains,
):
    cube = Cube()
    width = states.shape[1]
    half = cube.streams // 2
    position = lax.axis_index("stream")
    is_words = position < half
    count = states.shape[0] // SLOT
    block = position % half * cube.replicas + lax.axis_index("dp")
    lengths = lax.dynamic_slice_in_dim(word_lengths, block * count, count)
    key_bias = jnp.where(jnp.arange(SLOT)[None, :] < lengths[:, None], 0.0, MASKED).reshape(-1, 1)
    no_bias = jnp.zeros_like(key_bias)
    self_bias = jnp.where(is_words, key_bias, no_bias)
    cross_bias = jnp.where(is_words, no_bias, key_bias)
    packed = PACK * SLOT
    keys = lax.broadcasted_iota(jnp.int32, (packed, 4 * packed), 0) // SLOT
    queries = lax.broadcasted_iota(jnp.int32, (packed, 4 * packed), 1) % packed // SLOT
    apart = jnp.where(keys == queries, 0.0, APART).astype(F32)

    unit = object_output.shape[1]
    feed_unit = object_down.shape[0] // 2

    def attention_shard(project, output):
        return [project.T, output.T]

    def feed_shards(up, down):
        up = up.T
        return [up[:feed_unit], down[:feed_unit]], [up[feed_unit:], down[feed_unit:]]

    def piece(rows):
        return jnp.concatenate(rows, axis=0)[None]

    gain_shard = jnp.concatenate([object_gains, layer_gains], axis=0)
    kinds, span = gain_shard.shape
    gain_rows = jnp.pad(gain_shard, ((0, 8 - kinds), (0, width - span)))
    object_shards = [
        attention_shard(object_project, object_output) + [gain_rows],
        *feed_shards(object_up, object_down),
    ]
    cross_rows = jnp.concatenate(attention_shard(cross_project, cross_output), axis=0)
    third = cross_rows.shape[0] // 3
    cross_shards = [cross_rows[i * third : (i + 1) * third] for i in range(3)]
    words_shards = [attention_shard(words_project, words_output), *feed_shards(words_up, words_down)]
    region_shards = [attention_shard(region_project, region_output), *feed_shards(region_up, region_down)]

    orders = [cube.order(turn) for turn in (1, 0, 2)]
    tables = [cube.table(order) for order in orders]
    first = [Gather(cube, piece(rows), piece(rows), order) for rows, order in zip(object_shards, orders)]
    second = []
    for words, region, cross, order in zip(words_shards, region_shards, cross_shards, orders):
        own = piece([jnp.where(is_words, w, r) for w, r in zip(words, region)] + [cross])
        other = piece([jnp.where(is_words, r, w) for w, r in zip(words, region)] + [cross])
        second.append(Gather(cube, own, other, order))

    def step(chains, *others):
        for chain in chains:
            chain.advance(*others)
        return [chain.got for chain in chains]

    for chain, mark in zip(second, step(first)):
        chain.advance(mark)
    marks = [chain.got for chain in second]
    others = cube.swap(after(states, *marks), cube.half)
    step(first)
    step(first)
    for _ in cube.inner[2:]:
        marks = step(first, *marks)
    later = step(first)
    step(second, *marks)
    for _ in cube.inner[2:]:
        step(second, *later)

    object_in, object_out, gain_pieces = place_weights(tables[:1], [first[0].pair()], [0], 8)
    object_feed = [part for chain in first[1:] for part in chain.pair()]
    gains = gain_pieces[:, :kinds, :span].transpose(1, 0, 2).reshape(kinds, width)
    self_gain = jnp.where(is_words, gains[3], gains[4])[None]
    feed_gain = jnp.where(is_words, gains[5], gains[6])[None]

    language = jnp.where(is_words, states, others)
    vision = jnp.where(is_words, others, states)

    ready = beside(vision, *second)
    one, one_saved = attention_block(
        ready, ready, object_in, object_out, gains[0:1], no_bias, apart, False
    )
    two, two_saved = feed_block(one, object_feed, feed_unit, gains[1:2])
    x = beside(jnp.where(is_words, language, two), *second)
    pairs = [chain.pair() for chain in second]
    cross_in, cross_out = place_weights(tables, pairs, [pairs[0][0].shape[1] - third] * 3)
    y = jnp.where(is_words, two, language)
    three, three_saved = attention_block(x, y, cross_in, cross_out, gains[2:3], cross_bias, apart, True)
    self_in, self_out = place_weights(tables[:1], pairs[:1], [0])
    self_feed = [part for pair in pairs[1:] for part in pair]
    four, four_saved = attention_block(
        three, three, self_in, self_out, self_gain, self_bias, apart, False
    )
    five, five_saved = feed_block(four, self_feed, feed_unit, feed_gain)

    side = is_words.astype(jnp.int32)[None]

    hidden, slope, normed, rate = five_saved
    branch, feed_terms, *pair, middle = feed_back(
        (cotangent, normed, rate, feed_gain), four, self_feed[:2], feed_unit, hidden, slope, 0
    )
    sb = Scatter(cube, *pair, orders[1])
    *pair, grad_four = feed_back((beside(middle, sb), branch), four, self_feed[2:], feed_unit, hidden, slope, 2)
    sc = Scatter(cube, *pair, orders[2])

    branch, dj, grad_three, self_terms = attention_block_backward(
        beside(grad_four, sb, sc), self_in, self_out, self_gain, four_saved
    )
    (pair,) = attention_weights(tables[:1], beside(dj, sc), three, three, branch, four_saved[2])
    sa = Scatter(cube, *pair, orders[0])

    branch, dj, grad_language, grad_two, cross_terms = attention_block_backward(
        beside(grad_three, sa, sb), cross_in, cross_out, gains[2:3], three_saved, side
    )
    (pair,) = attention_weights(tables[:1], beside(dj, sa, sc, sb), x, y, branch, three_saved[2])
    xa = Scatter(cube, *pair, orders[0])

    hidden, slope, normed, rate = two_saved
    branch, two_terms, *pair, middle = feed_back(
        (beside(grad_two, xa, sb, sc), normed, rate, gains[1:2]), one, object_feed[:2], feed_unit, hidden, slope, 0
    )
    ob = Scatter(cube, *pair, orders[1])
    *pair, grad_one = feed_back(
        (beside(middle, ob, sa, sb, sc, xa), branch), one, object_feed[2:], feed_unit, hidden, slope, 2
    )
    oc = Scatter(cube, *pair, orders[2])
    branch, dj, grad_vision, one_terms = attention_block_backward(
        beside(grad_one, oc, ob, sa, sc, xa), object_in, object_out, gains[0:1], one_saved
    )
    words_side = is_words.astype(F32)
    region_side = 1.0 - words_side
    sums = [one_terms, two_terms, cross_terms, self_terms, self_terms, feed_terms, feed_terms]
    sides = [1.0, 1.0, 1.0, words_side, region_side, words_side, region_side]
    gain_sums = jnp.stack([jnp.sum(s, axis=0) * side for s, side in zip(sums, sides)])
    gain_cut = gain_sums.reshape(kinds, -1, span).transpose(1, 0, 2)
    gain_cut = jnp.pad(gain_cut, ((0, 0), (0, 8 - kinds), (0, width - span)))
    *others, last = cube.inner
    orders = [[last] + others, [last] + others[::-1], [last] + others]
    tables = [cube.table(order) for order in orders]
    pairs = attention_weights(
        tables, beside(dj, ob, oc, sa, xa), ready, ready, branch, one_saved[2], gain_cut
    )
    oas = [Scatter(cube, *pair, order) for pair, order in zip(pairs, orders)]
    step(oas)
    step([oc])
    step(oas)
    step([ob])
    step(oas)
    step([oc])
    last = step(oas)
    sent = jnp.where(is_words, grad_vision, grad_language).astype(BF)
    received = after(cube.swap(sent, cube.half), *last).astype(F32)
    grad_states = jnp.where(is_words, grad_language, grad_vision) + received

    def both(chain):
        own, other = chain.finish(*last)
        return own + other

    def apart_by_stream(chain):
        own, other = chain.finish(*last)
        return jnp.where(is_words, own, other), jnp.where(is_words, other, own)

    def attention_grads(piece):
        rows = flat(piece)
        return rows[: 3 * unit].T, rows[3 * unit : 4 * unit].T

    def feed_grads(first, second):
        joined = jnp.concatenate([first, second], axis=2)
        return joined[0, 0].T, joined[0, 1]

    object_parts = [both(chain) for chain in oas]
    more = object_parts[0].shape[1] - 1
    gain_grad = object_parts[0][0, more, :kinds, :span]
    object_piece = jnp.concatenate([object_parts[0][:, :more], *object_parts[1:]], axis=1)
    object_project_grad, object_output_grad = attention_grads(object_piece)
    object_up_grad, object_down_grad = feed_grads(both(ob), both(oc))
    cross_project_grad, cross_output_grad = attention_grads(both(xa))
    words_piece, region_piece = apart_by_stream(sa)
    words_project_grad, words_output_grad = attention_grads(words_piece)
    region_project_grad, region_output_grad = attention_grads(region_piece)
    split = [apart_by_stream(s) for s in (sb, sc)]
    words_up_grad, words_down_grad = feed_grads(split[0][0], split[1][0])
    region_up_grad, region_down_grad = feed_grads(split[0][1], split[1][1])
    return (
        five,
        grad_states,
        object_project_grad,
        object_output_grad,
        object_up_grad,
        object_down_grad,
        gain_grad[:2],
        cross_project_grad,
        cross_output_grad,
        words_project_grad,
        words_output_grad,
        region_project_grad,
        region_output_grad,
        words_up_grad,
        words_down_grad,
        region_up_grad,
        region_down_grad,
        gain_grad[2:],
    )


def solution(mesh):
    rows = P(("stream", "dp"), None)
    columns = P(None, ("stream", "dp"))
    in_specs = (
        rows, rows, P(),
        columns, columns, columns, rows, columns,
        columns, columns,
        columns, columns, columns, columns,
        columns, rows, columns, rows,
        columns,
    )
    out_specs = (
        rows, rows,
        columns, columns, columns, rows, columns,
        columns, columns,
        columns, columns, columns, columns,
        columns, rows, columns, rows,
        columns,
    )
    return jax.shard_map(
        on_device, mesh=mesh, in_specs=in_specs, out_specs=out_specs, check_vma=False
    )
```

```python
import functools

import jax
import jax.numpy as jnp
from jax import lax
from jax.experimental import pallas as pl
from jax.experimental.pallas import tpu as pltpu
from jax.sharding import PartitionSpec as P

HEADS = 12
SLOT = 36
PACK = 4
EPSILON = 1e-06
MASKED = -1000000000.0
APART = -1e30
BF = jnp.bfloat16
F32 = jnp.float32
VMEM_LIMIT = 48 * 1024 * 1024

NN = (((1,), (0,)), ((), ()))
NT = (((1,), (1,)), ((), ()))
TN = (((0,), (0,)), ((), ()))


def mm(left, right, dims):
    return lax.dot_general(left, right, dims, preferred_element_type=F32)


def norm_forward(total):
    center = total - jnp.mean(total, axis=-1, keepdims=True)
    spread = jnp.mean(center * center, axis=-1, keepdims=True)
    rate = lax.rsqrt(spread + EPSILON)
    return center * rate, rate


def norm_backward(grad, normed, rate, gain):
    slope = grad * gain
    first = jnp.mean(slope, axis=-1, keepdims=True)
    second = jnp.mean(slope * normed, axis=-1, keepdims=True)
    terms = grad * normed
    rows, width = terms.shape
    return rate * (slope - first - normed * second), jnp.sum(
        terms.reshape(rows // 8, 8, width), axis=0
    )


def gelu_pair(value):
    size = jnp.abs(value) * 0.7071067811865476
    t = 1.0 / (1.0 + 0.3275911 * size)
    bell = jnp.exp(-size * size)
    poly = t * (
        0.254829592
        + t * (-0.284496736 + t * (1.421413741 + t * (-1.453152027 + t * 1.061405429)))
    )
    tail = 0.5 * poly * bell
    phi = jnp.where(value >= 0.0, 1.0 - tail, tail)
    return value * phi, phi + value * bell * 0.3989422804014327


def head_masks(width, head):
    lane = lax.broadcasted_iota(jnp.int32, (1, width), 1)
    return [jnp.where(lane // head == i, 1.0, 0.0).astype(F32) for i in range(width // head)]


def spread_heads(block, masks):
    return jnp.concatenate([block * mask.astype(block.dtype) for mask in masks], axis=0)


def fold_heads(stacked, masks):
    rows = stacked.shape[0] // len(masks)
    total = stacked[:rows] * masks[0]
    for i in range(1, len(masks)):
        total = total + stacked[i * rows : (i + 1) * rows] * masks[i]
    return total


def attend_kernel(cross, x_ref, y_ref, p_ref, o_ref, g_ref, kb_ref, apart_ref,
                  out_ref, joined_ref, probs_ref, context_ref, normed_ref, rate_ref):
    x = x_ref[...]
    width = x.shape[1]
    head = width // HEADS
    quad = 4 * head
    scale = head ** (-0.5)
    if cross:
        joined_ref[:, :width] = mm(x, p_ref[:width], NT).astype(BF)
        joined_ref[:, width:] = mm(y_ref[...], p_ref[width:], NT).astype(BF)
    else:
        joined_ref[...] = mm(x, p_ref[...], NT).astype(BF)
    masks = head_masks(quad, head)
    group = PACK * SLOT
    for g in range(x.shape[0] // group):
        rows = slice(g * group, (g + 1) * group)
        bias = apart_ref[...] + kb_ref[rows]
        for i in range(width // quad):
            q = joined_ref[rows, i * quad : (i + 1) * quad]
            k = joined_ref[rows, width + i * quad : width + (i + 1) * quad]
            v = joined_ref[rows, 2 * width + i * quad : 2 * width + (i + 1) * quad]
            scores = mm(k, spread_heads(q, masks), NT) * scale + bias
            raised = jnp.exp(scores - jnp.max(scores, axis=0, keepdims=True))
            probs = (raised * (1.0 / jnp.sum(raised, axis=0, keepdims=True))).astype(BF)
            probs_ref[g, i] = probs
            context_ref[rows, i * quad : (i + 1) * quad] = fold_heads(mm(probs, v, TN), masks).astype(BF)
    total = x.astype(F32) + mm(context_ref[...], o_ref[...], NT)
    normed, rate = norm_forward(total)
    out_ref[...] = (normed * g_ref[...]).astype(BF)
    normed_ref[...] = normed.astype(BF)
    rate_ref[...] = rate


def whole(shape):
    return pl.BlockSpec(shape, lambda *_: (0,) * len(shape))


def in_vmem(shape):
    return pl.BlockSpec(shape, lambda: (0,) * len(shape))


def attention_block(x, y, project, output, gain, key_bias, apart, cross):
    rows, width = x.shape
    group = PACK * SLOT
    groups = rows // group
    steps = groups // 2 if groups % 2 == 0 else groups
    block = rows // steps
    quads = HEADS // 4
    probs_block = pl.BlockSpec((groups // steps, quads, group, 4 * group), lambda i: (i, 0, 0, 0))
    row = lambda w: pl.BlockSpec((block, w), lambda i: (i, 0))
    out, joined, probs, context, normed, rate = pl.pallas_call(
        functools.partial(attend_kernel, cross),
        grid=(steps,),
        in_specs=[
            row(width), row(width), whole(project.shape), whole(output.shape), whole((1, width)),
            row(1), whole(apart.shape),
        ],
        out_specs=[
            row(width), row(3 * width),
            probs_block,
            row(width), row(width), row(1),
        ],
        out_shape=[
            jax.ShapeDtypeStruct((rows, width), BF),
            jax.ShapeDtypeStruct((rows, 3 * width), BF),
            jax.ShapeDtypeStruct((groups, quads, group, 4 * group), BF),
            jax.ShapeDtypeStruct((rows, width), BF),
            jax.ShapeDtypeStruct((rows, width), BF),
            jax.ShapeDtypeStruct((rows, 1), F32),
        ],
        compiler_params=pltpu.CompilerParams(vmem_limit_bytes=VMEM_LIMIT),
        cost_estimate=pl.CostEstimate(
            flops=2 * rows * width * 6 * width, bytes_accessed=24 * rows * width, transcendentals=0
        ),
        name="attend",
    )(x, y, project, output, gain, key_bias, apart)
    return out, (joined, probs, context, normed, rate)


def attend_back_kernel(cross, grad_ref, normed_ref, rate_ref, g_ref, joined_ref, probs_ref, p_ref, o_ref,
                       *rest):
    if cross:
        side_ref, branch_ref, dj_ref, dx_ref, dy_ref, gain_ref = rest
    else:
        branch_ref, dj_ref, dx_ref, gain_ref = rest
    width = grad_ref.shape[1]
    head = width // HEADS
    quad = 4 * head
    scale = head ** (-0.5)
    total, terms = norm_backward(
        grad_ref[...].astype(F32), normed_ref[...].astype(F32), rate_ref[...], g_ref[...]
    )

    @pl.when(pl.program_id(0) == 0)
    def _():
        gain_ref[...] = jnp.zeros_like(gain_ref)

    gain_ref[...] += terms
    branch = total.astype(BF)
    branch_ref[...] = branch
    grad_context = mm(branch, o_ref[...], NN).astype(BF)
    masks = head_masks(quad, head)
    group = PACK * SLOT
    for g in range(grad_context.shape[0] // group):
        rows = slice(g * group, (g + 1) * group)
        for i in range(width // quad):
            low, high = i * quad, (i + 1) * quad
            q = joined_ref[rows, low:high]
            k = joined_ref[rows, width + low : width + high]
            v = joined_ref[rows, 2 * width + low : 2 * width + high]
            probs = probs_ref[g, i]
            wide = probs.astype(F32)
            grad_heads = spread_heads(grad_context[rows, low:high], masks)
            grad_probs = mm(v, grad_heads, NT)
            mean = jnp.sum(wide * grad_probs, axis=0, keepdims=True)
            grad_scores = (wide * (grad_probs - mean)).astype(BF)
            dj_ref[rows, low:high] = (fold_heads(mm(grad_scores, k, TN), masks) * scale).astype(BF)
            dj_ref[rows, width + low : width + high] = (
                mm(grad_scores, spread_heads(q, masks), NN) * scale
            ).astype(BF)
            dj_ref[rows, 2 * width + low : 2 * width + high] = mm(probs, grad_heads, NN).astype(BF)
    if cross:
        dx = total + mm(dj_ref[:, :width], p_ref[:width], NN)
        dy = mm(dj_ref[:, width:], p_ref[width:], NN)
        words = side_ref[0] == 1
        dx_ref[...] = jnp.where(words, dx, dy)
        dy_ref[...] = jnp.where(words, dy, dx)
    else:
        dx_ref[...] = total + mm(dj_ref[...], p_ref[...], NN)


def attention_block_backward(grad, project, output, gain, saved, side=None):
    cross = side is not None
    joined, probs, context, normed, rate = saved
    rows, width = normed.shape
    group = PACK * SLOT
    groups = rows // group
    steps = groups // 2 if groups % 2 == 0 else groups
    block = rows // steps
    quads = HEADS // 4
    probs_block = pl.BlockSpec((groups // steps, quads, group, 4 * group), lambda i: (i, 0, 0, 0))
    row = lambda w: pl.BlockSpec((block, w), lambda i: (i, 0))
    extra_spec = [row(width)] if cross else []
    extra_shape = [jax.ShapeDtypeStruct((rows, width), F32)] if cross else []
    return pl.pallas_call(
        functools.partial(attend_back_kernel, cross),
        grid=(steps,),
        in_specs=[
            row(width), row(width), row(1), whole((1, width)), row(3 * width),
            probs_block,
            whole(project.shape), whole(output.shape),
        ]
        + [pl.BlockSpec(memory_space=pltpu.SMEM)] * cross,
        out_specs=[row(width), row(3 * width), row(width)] + extra_spec + [whole((8, width))],
        out_shape=[
            jax.ShapeDtypeStruct((rows, width), BF),
            jax.ShapeDtypeStruct((rows, 3 * width), BF),
            jax.ShapeDtypeStruct((rows, width), F32),
        ]
        + extra_shape
        + [jax.ShapeDtypeStruct((8, width), F32)],
        compiler_params=pltpu.CompilerParams(vmem_limit_bytes=VMEM_LIMIT),
        cost_estimate=pl.CostEstimate(
            flops=2 * rows * width * 7 * width, bytes_accessed=32 * rows * width, transcendentals=0
        ),
        name="attend_back",
    )(grad, normed, rate, gain, joined, probs, project, output, *([side] if cross else []))


def attend_weights_kernel(parts, extra, *refs):
    tables, (dj_ref, x_ref, y_ref, branch_ref, context_ref) = refs[:parts], refs[parts : parts + 5]
    extra_ref = refs[parts + 5] if extra else None
    outputs, total = refs[parts + 5 + extra : -1], refs[-1]
    width = x_ref.shape[1]
    total[:width] = mm(dj_ref[:, :width], x_ref[...], TN)
    total[width : 3 * width] = mm(dj_ref[:, width:], y_ref[...], TN)
    total[3 * width :] = mm(branch_ref[...], context_ref[...], TN)
    for part in range(parts):
        mine_ref, theirs_ref = outputs[2 * part : 2 * part + 2]
        count = mine_ref.shape[0]
        unit = width // (2 * count)
        first, last = part * 4 * unit // parts, (part + 1) * 4 * unit // parts

        def take(i, carry):
            for target, offset in ((mine_ref, 0), (theirs_ref, count)):
                at = tables[part][offset + i]
                filled = 0
                for start, size, base in ((0, 3 * unit, 0), (3 * unit, unit, 3 * width)):
                    low, high = max(first, start), min(last, start + size)
                    if low < high:
                        row = pl.multiple_of(base + at * size + low - start, 8)
                        block = total[pl.ds(row, high - low)].reshape(-1, 8, width)
                        target[i, filled : filled + block.shape[0]] = block.astype(BF)
                        filled += block.shape[0]
                if extra and part == 0:
                    target[i, filled] = extra_ref[at].astype(BF)
            return carry

        lax.fori_loop(0, count, take, 0)


def attention_weights(tables, dj, x, y, branch, context, extra=None):
    rows, width = x.shape
    count = tables[0].shape[0] // 2
    unit = width // (2 * count)
    parts = len(tables)
    units = 4 * unit // 8 // parts
    if unit % 8:
        project = jnp.concatenate([mm(dj[:, :width], x, TN), mm(dj[:, width:], y, TN)], axis=0)
        project = project.astype(BF).reshape(2 * count, 3 * unit, width)
        output = mm(branch, context, TN).astype(BF).reshape(2 * count, unit, width)
        joined = jnp.concatenate([project, output], axis=1).reshape(2 * count, units * parts, 8, width)
        pairs = []
        for part, table in enumerate(tables):
            piece = joined[:, part * units : (part + 1) * units]
            if extra is not None and part == 0:
                piece = jnp.concatenate([piece, extra[:, None].astype(BF)], axis=1)
            piece = piece[table]
            pairs.append((piece[:count], piece[count:]))
        return pairs
    more = [] if extra is None else [extra]
    shapes = [(count, units + (len(more) if part == 0 else 0), 8, width) for part in range(parts) for _ in (0, 1)]
    outputs = pl.pallas_call(
        functools.partial(attend_weights_kernel, parts, len(more)),
        in_specs=[pl.BlockSpec(memory_space=pltpu.SMEM)] * parts
        + [in_vmem(a.shape) for a in (dj, x, y, branch, context, *more)],
        out_specs=[in_vmem(shape) for shape in shapes],
        out_shape=[jax.ShapeDtypeStruct(shape, BF) for shape in shapes],
        scratch_shapes=[pltpu.VMEM((4 * width, width), F32)],
        compiler_params=pltpu.CompilerParams(vmem_limit_bytes=VMEM_LIMIT),
        cost_estimate=pl.CostEstimate(
            flops=2 * rows * width * 4 * width, bytes_accessed=16 * rows * width, transcendentals=0
        ),
        name="attend_weights",
    )(*tables, dj, x, y, branch, context, *more)
    return [tuple(outputs[2 * part : 2 * part + 2]) for part in range(parts)]


def flat(block):
    return block.reshape(-1, block.shape[-1])


def feed_operands(weight, unit, steps):
    pieces, _, width = weight.shape
    if unit % 16 == 0:
        block = (pieces // steps, unit, width)
        return [weight, weight], [
            pl.BlockSpec(block, lambda s: (s % steps, 0, 0)),
            pl.BlockSpec(block, lambda s: (s % steps, 1, 0)),
        ]
    arrays = [weight[:, i * unit : (i + 1) * unit].reshape(steps, -1, width) for i in (0, 1)]
    return arrays, [pl.BlockSpec((1,) + arrays[0].shape[1:], lambda s: (s % steps, 0, 0))] * 2


def feed_kernel(x_ref, *refs):
    weights, (g_ref, out_ref, hidden_ref, slope_ref, normed_ref, rate_ref) = refs[:8], refs[8:]
    x = x_ref[...]
    wide = weights[0].shape[0] * weights[0].shape[1]
    total = x.astype(F32)
    for i in range(4):
        hidden, slope = gelu_pair(mm(x, flat(weights[2 * i][...]), NT))
        hidden = hidden.astype(BF)
        hidden_ref[:, i * wide : (i + 1) * wide] = hidden
        slope_ref[:, i * wide : (i + 1) * wide] = slope.astype(BF)
        total = total + mm(hidden, flat(weights[2 * i + 1][...]), NN)
    normed, rate = norm_forward(total)
    out_ref[...] = (normed * g_ref[...]).astype(BF)
    normed_ref[...] = normed.astype(BF)
    rate_ref[...] = rate


def feed_block(x, weights, unit, gain):
    rows, width = x.shape
    hidden = weights[0].shape[0] * unit * len(weights)
    parts = [feed_operands(weight, unit, 1) for weight in weights]
    block = rows // 3
    row = lambda w: pl.BlockSpec((block, w), lambda i: (i, 0))
    out, *saved = pl.pallas_call(
        feed_kernel,
        grid=(rows // block,),
        in_specs=[row(width)] + [spec for _, specs in parts for spec in specs] + [whole((1, width))],
        out_specs=[row(width), row(hidden), row(hidden), row(width), row(1)],
        out_shape=[
            jax.ShapeDtypeStruct((rows, width), BF),
            jax.ShapeDtypeStruct((rows, hidden), BF),
            jax.ShapeDtypeStruct((rows, hidden), BF),
            jax.ShapeDtypeStruct((rows, width), BF),
            jax.ShapeDtypeStruct((rows, 1), F32),
        ],
        compiler_params=pltpu.CompilerParams(vmem_limit_bytes=VMEM_LIMIT),
        cost_estimate=pl.CostEstimate(
            flops=4 * rows * width * hidden, bytes_accessed=4 * (rows + width) * hidden, transcendentals=0
        ),
        name="feed",
    )(x, *[array for arrays, _ in parts for array in arrays], gain)
    return out, tuple(saved)


def feed_back_kernel(first, *refs):
    if first:
        grad_ref, normed_ref, rate_ref, g_ref, x_ref, *refs = refs
        inputs, (branch_ref, gain_ref, *outputs) = refs[:8], refs[8:]
    else:
        start_ref, branch_ref, x_ref, *refs = refs
        inputs, outputs = refs[:8], refs[8:]
    dx_ref = outputs[-1]

    @pl.when(pl.program_id(0) == 0)
    def _():
        if first:
            total, gain_ref[...] = norm_backward(
                grad_ref[...].astype(F32), normed_ref[...].astype(F32), rate_ref[...], g_ref[...]
            )
            dx_ref[...] = total
            branch_ref[...] = total.astype(BF)
        else:
            dx_ref[...] = start_ref[...]

    branch = branch_ref[...]
    x = x_ref[...]
    for i in range(2):
        up_ref, down_ref, hidden_ref, slope_ref = inputs[4 * i : 4 * i + 4]
        grad_ref = outputs[i]
        pieces, _, unit, width = grad_ref.shape
        grad_hidden = mm(branch, flat(down_ref[...]), NT)
        grad_raised = (grad_hidden * slope_ref[...].astype(F32)).astype(BF)
        grad_ref[:, 0] = mm(grad_raised, x, TN).astype(BF).reshape(pieces, unit, width)
        grad_ref[:, 1] = mm(hidden_ref[...], branch, TN).astype(BF).reshape(pieces, unit, width)
        dx_ref[...] += mm(grad_raised, flat(up_ref[...]), NN)


def feed_back(start, x, weights, unit, hidden, slope, quarter):
    rows, width = x.shape
    first = len(start) == 4
    pieces = weights[0].shape[0]
    steps = 2 if pieces * unit // 2 % 128 == 0 else 1
    tile = pieces * unit // steps
    specs = [whole(a.shape) for a in (*start, x)]
    operands = [*start, x]
    cut = pl.BlockSpec((pieces // steps, 2, unit, width), lambda s: (s, 0, 0, 0))
    for i, weight in enumerate(weights):
        columns = pl.BlockSpec((rows, tile), lambda s, base=(quarter + i) * steps: (0, base + s))
        arrays, blocks = feed_operands(weight, unit, steps)
        specs += [*blocks, columns, columns]
        operands += [*arrays, hidden, slope]
    out_specs = [cut, cut, whole((rows, width))]
    out_shape = [jax.ShapeDtypeStruct((pieces, 2, unit, width), BF)] * 2
    out_shape += [jax.ShapeDtypeStruct((rows, width), F32)]
    if first:
        out_specs = [whole((rows, width)), whole((8, width))] + out_specs
        out_shape = [jax.ShapeDtypeStruct((rows, width), BF), jax.ShapeDtypeStruct((8, width), F32)] + out_shape
    return pl.pallas_call(
        functools.partial(feed_back_kernel, first),
        grid=(steps,),
        in_specs=specs,
        out_specs=out_specs,
        out_shape=out_shape,
        compiler_params=pltpu.CompilerParams(vmem_limit_bytes=VMEM_LIMIT),
        cost_estimate=pl.CostEstimate(
            flops=16 * rows * width * pieces * unit, bytes_accessed=30 * pieces * unit * width, transcendentals=0
        ),
        name="feed_back",
    )(*operands)


def place_kernel(parts, rows, extra, *refs):
    tables, sources, (p_ref, o_ref, *more) = refs[:parts], refs[parts : 3 * parts], refs[3 * parts :]
    count = sources[0].shape[0]
    unit = o_ref.shape[1]

    def put(device, carry):
        found = []
        for part in range(parts):
            mine_ref, theirs_ref = sources[2 * part : 2 * part + 2]
            at = tables[part][device]
            mine = mine_ref[jnp.minimum(at, count - 1)].astype(F32)
            theirs = theirs_ref[jnp.maximum(at - count, 0)].astype(F32)
            found.append(jnp.where(at < count, mine, theirs))
        piece = found[0] if parts == 1 else jnp.concatenate(found, axis=0)
        p_ref[device] = piece[: 3 * unit].astype(BF)
        o_ref[device] = piece[3 * unit : 4 * unit].astype(BF)
        if extra:
            more[0][device] = piece[4 * unit :]
        return carry

    lax.fori_loop(0, 2 * count, put, 0)


def place_weights(tables, pairs, skip, extra=0):
    parts = len(pairs)
    count, _, width = pairs[0][0].shape
    unit = width // (2 * count)
    rows = 4 * unit // parts + extra
    places = [jnp.argsort(table) for table in tables]
    if unit % 8:
        pieces = [
            jnp.concatenate(pair, axis=0)[place, skip : skip + rows]
            for pair, place, skip in zip(pairs, places, skip)
        ]
        joined = jnp.concatenate(pieces, axis=1)
        made = [joined[:, : 3 * unit], joined[:, 3 * unit : 4 * unit], joined[:, 4 * unit :].astype(F32)]
    else:
        shapes = [(2 * count, 3 * unit, width), (2 * count, unit, width)] + [(2 * count, extra, width)] * (extra > 0)
        specs = []
        for offset in skip:
            block = pl.BlockSpec((count, rows, width), lambda i, at=offset // rows: (0, at, 0))
            specs += [block, block]
        made = pl.pallas_call(
            functools.partial(place_kernel, parts, rows, extra),
            grid=(1,),
            in_specs=[pl.BlockSpec(memory_space=pltpu.SMEM)] * parts + specs,
            out_specs=[whole(shape) for shape in shapes],
            out_shape=[jax.ShapeDtypeStruct(shape, F32 if i == 2 else BF) for i, shape in enumerate(shapes)],
            compiler_params=pltpu.CompilerParams(vmem_limit_bytes=VMEM_LIMIT),
            cost_estimate=pl.CostEstimate(flops=0, bytes_accessed=16 * width * width, transcendentals=0),
            name="place",
        )(*places, *[piece for pair in pairs for piece in pair])
    project, output = made[0].reshape(-1, width), made[1].reshape(-1, width)
    return (project, output, made[2]) if extra else (project, output)


class Cube:
    def __init__(self):
        self.replicas = lax.axis_size("dp")
        self.streams = lax.axis_size("stream")
        low = self.replicas.bit_length() - 1
        bits = low + self.streams.bit_length() - 1
        self.half = bits - 1
        self.core = low
        self.inner = [b for b in range(bits) if b not in (self.half, self.core)]
        self.number = lax.axis_index("stream") * self.replicas + lax.axis_index("dp")

    def swap(self, value, bit):
        step = 1 << bit
        if step < self.replicas:
            return lax.ppermute(value, "dp", [(i, i ^ step) for i in range(self.replicas)])
        step //= self.replicas
        return lax.ppermute(value, "stream", [(i, i ^ step) for i in range(self.streams)])

    def order(self, turn):
        turn %= len(self.inner)
        return self.inner[turn:] + self.inner[:turn]

    def pieces(self, stages):
        order = stages[::-1]
        relative = [
            sum(1 << bit for place, bit in enumerate(order) if i >> place & 1) for i in range(1 << len(order))
        ]
        return self.number ^ jnp.array(relative, jnp.int32)

    def table(self, order):
        return self.pieces([self.core] + order[::-1] + [self.half])


def after(value, *others):
    return lax.optimization_barrier((value,) + others)[0]


class Gather:
    def __init__(self, cube, own, other, order):
        self.cube, self.pieces = cube, own
        self.stages = [cube.half] + order + [cube.core]
        self.sent, self.got, self.done = other, None, 0

    def advance(self, *others):
        if self.done:
            pieces, got = self.pieces, self.got
            if others:
                pieces, got, *_ = lax.optimization_barrier((pieces, got, *others))
            self.sent = self.pieces = jnp.concatenate([pieces, got], axis=0)
        elif others:
            self.sent = after(self.sent, *others)
        self.got = self.cube.swap(self.sent, self.stages[self.done])
        self.done += 1

    def pair(self):
        return self.pieces, self.got


class Scatter:
    def __init__(self, cube, keep, send, order):
        self.cube = cube
        self.stages = [cube.core] + order[::-1] + [cube.half]
        self.kept, self.sent, self.got, self.done = keep, send, None, 0

    def advance(self, *others):
        if self.done:
            kept, got = self.kept, self.got
            if others:
                kept, got, *_ = lax.optimization_barrier((kept, got, *others))
            if self.done == len(self.stages):
                self.kept, self.got, self.sent = kept, got, got
                return
            count = kept.shape[0] // 2
            self.sent = add(kept[count:], got[count:])
            self.kept = add(kept[:count], got[:count])
        self.got = self.cube.swap(self.sent, self.stages[self.done])
        self.done += 1

    def finish(self, *others):
        while self.done < len(self.stages):
            self.advance()
        self.advance(*others)
        return self.kept.astype(F32), self.got.astype(F32)


def beside(value, *chains):
    for chain in chains:
        chain.advance(value)
    return after(value, *[chain.sent for chain in chains])


def add(left, right):
    return (left.astype(F32) + right.astype(F32)).astype(left.dtype)


def on_device(
    states,
    cotangent,
    word_lengths,
    object_project,
    object_output,
    object_up,
    object_down,
    object_gains,
    cross_project,
    cross_output,
    words_project,
    words_output,
    region_project,
    region_output,
    words_up,
    words_down,
    region_up,
    region_down,
    layer_gains,
):
    cube = Cube()
    width = states.shape[1]
    half = cube.streams // 2
    position = lax.axis_index("stream")
    is_words = position < half
    count = states.shape[0] // SLOT
    block = position % half * cube.replicas + lax.axis_index("dp")
    lengths = lax.dynamic_slice_in_dim(word_lengths, block * count, count)
    key_bias = jnp.where(jnp.arange(SLOT)[None, :] < lengths[:, None], 0.0, MASKED).reshape(-1, 1)
    no_bias = jnp.zeros_like(key_bias)
    self_bias = jnp.where(is_words, key_bias, no_bias)
    cross_bias = jnp.where(is_words, no_bias, key_bias)
    packed = PACK * SLOT
    keys = lax.broadcasted_iota(jnp.int32, (packed, 4 * packed), 0) // SLOT
    queries = lax.broadcasted_iota(jnp.int32, (packed, 4 * packed), 1) % packed // SLOT
    apart = jnp.where(keys == queries, 0.0, APART).astype(F32)

    unit = object_output.shape[1]
    feed_unit = object_down.shape[0] // 2

    def attention_shard(project, output):
        return [project.T, output.T]

    def feed_shards(up, down):
        up = up.T
        return [up[:feed_unit], down[:feed_unit]], [up[feed_unit:], down[feed_unit:]]

    def piece(rows):
        return jnp.concatenate(rows, axis=0)[None]

    gain_shard = jnp.concatenate([object_gains, layer_gains], axis=0)
    kinds, span = gain_shard.shape
    gain_rows = jnp.pad(gain_shard, ((0, 8 - kinds), (0, width - span)))
    object_shards = [
        attention_shard(object_project, object_output) + [gain_rows],
        *feed_shards(object_up, object_down),
    ]
    cross_rows = jnp.concatenate(attention_shard(cross_project, cross_output), axis=0)
    third = cross_rows.shape[0] // 3
    cross_shards = [cross_rows[i * third : (i + 1) * third] for i in range(3)]
    words_shards = [attention_shard(words_project, words_output), *feed_shards(words_up, words_down)]
    region_shards = [attention_shard(region_project, region_output), *feed_shards(region_up, region_down)]

    orders = [cube.order(turn) for turn in (1, 0, 2)]
    tables = [cube.table(order) for order in orders]
    first = [Gather(cube, piece(rows), piece(rows), order) for rows, order in zip(object_shards, orders)]
    second = []
    for words, region, cross, order in zip(words_shards, region_shards, cross_shards, orders):
        own = piece([jnp.where(is_words, w, r) for w, r in zip(words, region)] + [cross])
        other = piece([jnp.where(is_words, r, w) for w, r in zip(words, region)] + [cross])
        second.append(Gather(cube, own, other, order))

    def step(chains, *others):
        for chain in chains:
            chain.advance(*others)
        return [chain.got for chain in chains]

    for chain, mark in zip(second, step(first)):
        chain.advance(mark)
    marks = [chain.got for chain in second]
    others = cube.swap(after(states, *marks), cube.half)
    step(first)
    step(first)
    for _ in cube.inner[2:]:
        marks = step(first, *marks)
    later = step(first)
    step(second, *marks)
    for _ in cube.inner[2:]:
        step(second, *later)

    object_in, object_out, gain_pieces = place_weights(tables[:1], [first[0].pair()], [0], 8)
    object_feed = [part for chain in first[1:] for part in chain.pair()]
    gains = gain_pieces[:, :kinds, :span].transpose(1, 0, 2).reshape(kinds, width)
    self_gain = jnp.where(is_words, gains[3], gains[4])[None]
    feed_gain = jnp.where(is_words, gains[5], gains[6])[None]

    language = jnp.where(is_words, states, others)
    vision = jnp.where(is_words, others, states)

    ready = vision
    one, one_saved = attention_block(
        ready, ready, object_in, object_out, gains[0:1], no_bias, apart, False
    )
    two, two_saved = feed_block(beside(one, *second), object_feed, feed_unit, gains[1:2])
    x = jnp.where(is_words, language, two)
    step(second, two)
    pairs = [chain.pair() for chain in second]
    cross_in, cross_out = place_weights(tables, pairs, [pairs[0][0].shape[1] - third] * 3)
    y = jnp.where(is_words, two, language)
    three, three_saved = attention_block(x, y, cross_in, cross_out, gains[2:3], cross_bias, apart, True)
    self_in, self_out = place_weights(tables[:1], pairs[:1], [0])
    self_feed = [part for pair in pairs[1:] for part in pair]
    four, four_saved = attention_block(
        three, three, self_in, self_out, self_gain, self_bias, apart, False
    )
    five, five_saved = feed_block(four, self_feed, feed_unit, feed_gain)

    side = is_words.astype(jnp.int32)[None]

    hidden, slope, normed, rate = five_saved
    branch, feed_terms, *pair, middle = feed_back(
        (cotangent, normed, rate, feed_gain), four, self_feed[:2], feed_unit, hidden, slope, 0
    )
    sb = Scatter(cube, *pair, orders[1])
    *pair, grad_four = feed_back((beside(middle, sb), branch), four, self_feed[2:], feed_unit, hidden, slope, 2)
    sc = Scatter(cube, *pair, orders[2])

    branch, dj, grad_three, self_terms = attention_block_backward(
        beside(grad_four, sb, sc), self_in, self_out, self_gain, four_saved
    )
    (pair,) = attention_weights(tables[:1], beside(dj, sc), three, three, branch, four_saved[2])
    sa = Scatter(cube, *pair, orders[0])

    branch, dj, grad_language, grad_two, cross_terms = attention_block_backward(
        beside(grad_three, sa, sb), cross_in, cross_out, gains[2:3], three_saved, side
    )
    (pair,) = attention_weights(tables[:1], beside(dj, sa, sc, sb), x, y, branch, three_saved[2])
    xa = Scatter(cube, *pair, orders[0])

    hidden, slope, normed, rate = two_saved
    branch, two_terms, *pair, middle = feed_back(
        (beside(grad_two, xa, sb, sc), normed, rate, gains[1:2]), one, object_feed[:2], feed_unit, hidden, slope, 0
    )
    ob = Scatter(cube, *pair, orders[1])
    *pair, grad_one = feed_back(
        (beside(middle, ob, sa, sb, sc, xa), branch), one, object_feed[2:], feed_unit, hidden, slope, 2
    )
    oc = Scatter(cube, *pair, orders[2])
    branch, dj, grad_vision, one_terms = attention_block_backward(
        beside(grad_one, oc, ob, sa, sc, xa), object_in, object_out, gains[0:1], one_saved
    )
    words_side = is_words.astype(F32)
    region_side = 1.0 - words_side
    sums = [one_terms, two_terms, cross_terms, self_terms, self_terms, feed_terms, feed_terms]
    sides = [1.0, 1.0, 1.0, words_side, region_side, words_side, region_side]
    gain_sums = jnp.stack([jnp.sum(s, axis=0) * side for s, side in zip(sums, sides)])
    gain_cut = gain_sums.reshape(kinds, -1, span).transpose(1, 0, 2)
    gain_cut = jnp.pad(gain_cut, ((0, 0), (0, 8 - kinds), (0, width - span)))
    *others, last = cube.inner
    orders = [[last] + others, [last] + others[::-1], [last] + others]
    tables = [cube.table(order) for order in orders]
    pairs = attention_weights(
        tables, beside(dj, ob, oc, sa, xa), ready, ready, branch, one_saved[2], gain_cut
    )
    oas = [Scatter(cube, *pair, order) for pair, order in zip(pairs, orders)]
    step(oas)
    step([oc])
    step(oas)
    step([ob])
    step(oas)
    step([oc])
    last = step(oas)
    sent = jnp.where(is_words, grad_vision, grad_language).astype(BF)
    received = after(cube.swap(sent, cube.half), *last).astype(F32)
    grad_states = jnp.where(is_words, grad_language, grad_vision) + received

    def both(chain):
        own, other = chain.finish(*last)
        return own + other

    def apart_by_stream(chain):
        own, other = chain.finish(*last)
        return jnp.where(is_words, own, other), jnp.where(is_words, other, own)

    def attention_grads(piece):
        rows = flat(piece)
        return rows[: 3 * unit].T, rows[3 * unit : 4 * unit].T

    def feed_grads(first, second):
        joined = jnp.concatenate([first, second], axis=2)
        return joined[0, 0].T, joined[0, 1]

    object_parts = [both(chain) for chain in oas]
    more = object_parts[0].shape[1] - 1
    gain_grad = object_parts[0][0, more, :kinds, :span]
    object_piece = jnp.concatenate([object_parts[0][:, :more], *object_parts[1:]], axis=1)
    object_project_grad, object_output_grad = attention_grads(object_piece)
    object_up_grad, object_down_grad = feed_grads(both(ob), both(oc))
    cross_project_grad, cross_output_grad = attention_grads(both(xa))
    words_piece, region_piece = apart_by_stream(sa)
    words_project_grad, words_output_grad = attention_grads(words_piece)
    region_project_grad, region_output_grad = attention_grads(region_piece)
    split = [apart_by_stream(s) for s in (sb, sc)]
    words_up_grad, words_down_grad = feed_grads(split[0][0], split[1][0])
    region_up_grad, region_down_grad = feed_grads(split[0][1], split[1][1])
    return (
        five,
        grad_states,
        object_project_grad,
        object_output_grad,
        object_up_grad,
        object_down_grad,
        gain_grad[:2],
        cross_project_grad,
        cross_output_grad,
        words_project_grad,
        words_output_grad,
        region_project_grad,
        region_output_grad,
        words_up_grad,
        words_down_grad,
        region_up_grad,
        region_down_grad,
        gain_grad[2:],
    )


def solution(mesh):
    rows = P(("stream", "dp"), None)
    columns = P(None, ("stream", "dp"))
    in_specs = (
        rows, rows, P(),
        columns, columns, columns, rows, columns,
        columns, columns,
        columns, columns, columns, columns,
        columns, rows, columns, rows,
        columns,
    )
    out_specs = (
        rows, rows,
        columns, columns, columns, rows, columns,
        columns, columns,
        columns, columns, columns, columns,
        columns, rows, columns, rows,
        columns,
    )
    return jax.shard_map(
        on_device, mesh=mesh, in_specs=in_specs, out_specs=out_specs, check_vma=False
    )
```
